128 devices in a mesh: tensor: 4 (over y_hi, core), context: 32 (over z, x, y_lo).
Axes of the slice: x: 4, y: 4 (y_hi: 2, y_lo: 2; y = y_hi * 2 + y_lo), z: 4, core: 2. Of those that a mesh axis runs over, the one named last changes fastest.
Arguments:
- queries: bfloat16 [4096, 8192], P('context', 'tensor'), may hold values from -80 to 80
- keys: bfloat16 [4096, 512], P('context', 'tensor'), may hold values from -4 to 4
- values: bfloat16 [4096, 512], P('context', 'tensor'), may hold values from -48 to 48
- resid: bfloat16 [4096, 4096], P(('context', 'tensor')), may hold values from -3 to 3
- out_weight: bfloat16 [8192, 4096], P('tensor', 'context'), may hold values from -0.0625 to 0.0625
- norm_gain: float32 [4096], replicated, may hold values from 0.1 to 1.9
- routes: int32 [4096, 8], P(('context', 'tensor')), may hold values from 0 to 63, all different within a row; in each aligned block of 32 rows (0 to 31, 32 to 63, ...) at most 6 rows name the same one
- gates: float32 [4096, 8], P(('context', 'tensor')), may hold values from 0.05 to 0.35
- w_gate: bfloat16 [64, 4096, 1536], P('context', None, 'tensor'), may hold values from -0.09375 to 0.09375
- w_up: bfloat16 [64, 4096, 1536], P('context', None, 'tensor'), may hold values from -0.09375 to 0.09375
- w_down: bfloat16 [64, 1536, 4096], P('context', 'tensor'), may hold values from -0.15625 to 0.15625
Outputs:
- mixed: bfloat16 [4096, 4096], P(('context', 'tensor'))
The draws below stay inside these ranges and needn't reach their ends.
Inputs may be any that keep to these rules, and one draw needn't show every extreme that they name: `routes`: each row names 8 different experts; in each aligned block of 32 rows (the rows of one device) no expert is named by more than 6 rows, a bound that some block reaches.
All inputs are finite; a program needn't handle non-finite values.
Results may differ from the reference program's by a relative error of at most 0.018.
Values may be sent and summed in bfloat16 or wider, within the bound.
A program may use at most 192 MiB of HBM per device.

```python
import math
import jax
import jax.numpy as jnp
import numpy as np
from jax import lax

D = 4096
FF = 1536
QUERY_HEADS = 64
KEY_VALUE_HEADS = 4
HEAD_WIDTH = 128
TOPK = 8
SEQUENCE_TOKENS = 4096
TOK_OWN = 32
EXPERTS = 64
CAP = 6
N_TENSOR = 4


def shared_keys(key):
    return jnp.clip(jax.random.normal(key, (SEQUENCE_TOKENS, KEY_VALUE_HEADS * HEAD_WIDTH), jnp.float32), -4.0, 4.0)


def draw_keys(key, part):
    group_offset = shared_keys(key)
    return group_offset.astype(jnp.bfloat16)


def draw_queries(key, part):
    key = jax.random.fold_in(key, 12)
    drawn = jnp.clip(jax.random.normal(key, (SEQUENCE_TOKENS, QUERY_HEADS * HEAD_WIDTH), jnp.float32), -4.0, 4.0)
    return drawn.astype(jnp.bfloat16)


def shard_levels(key, dims, split, low, high):
    loudness, own = 1.0, jax.random.fold_in(key, 6)
    for axis_at, shards_of in split:
        draws = jnp.exp(jax.random.uniform(jax.random.fold_in(own, axis_at), (shards_of,), jnp.float32, low / len(split), high / len(split)))
        loudness = loudness * jnp.repeat(draws, dims[axis_at] // shards_of).reshape([-1 if axis == axis_at else 1 for axis in range(len(dims))])
    return loudness


def shared_out(rng, own, number, rows, number_of, top, bound, slope):
    order = jax.random.permutation(rng, number_of)
    packed, usual = shares(number_of, rows * top, bound, slope, True), shares(number_of, rows * top, bound, slope, False)
    places = jnp.arange(number_of)

    def named(tallies, turn):
        used = int((tallies > 0).sum())
        fixed = max(1, used // 4)
        shifted = fixed + (places - fixed + turn * (used - fixed)) % max(1, number_of - fixed)
        return jnp.zeros((number_of,), jnp.int32).at[order[jnp.where(places < fixed, places, shifted)]].set(jnp.asarray(tallies, jnp.int32))

    tallies = jnp.where(number % 4 == 0, named(packed, number // 4), named(usual, number - number // 4 - 1))
    mixed = jax.random.permutation(jax.random.fold_in(own, 3), number_of)
    giver, receiver = mixed[0:number_of // 2 * 2:2], mixed[1:number_of // 2 * 2:2]
    margin = jnp.minimum(tallies[giver] - 1, bound - tallies[receiver]) // 2
    margin = jnp.where((giver == order[0]) | (receiver == order[0]) | (tallies[receiver] == 0), 0, jnp.maximum(margin, 0))
    shifted = jax.random.randint(jax.random.fold_in(own, 4), (number_of // 2,), 0, 1 << 20) % (margin + 1)
    tallies = tallies.at[giver].add(-shifted).at[receiver].add(shifted)
    items = jnp.searchsorted(jnp.cumsum(tallies), jnp.arange(rows * top), side="right").astype(jnp.int32)
    grid = items.reshape(top, rows).T
    grid = grid[jax.random.permutation(jax.random.fold_in(own, 1), rows)]
    turn = jax.random.randint(jax.random.fold_in(own, 2), (rows, 1), 0, top)
    return jnp.take_along_axis(grid, (jnp.arange(top)[None, :] + turn) % top, axis=1)


def shares(count, total, limit, slope, full):
    loads = [(1 << 20) // math.isqrt(grade ** slope) + 1 for grade in range(1, count + 1)]
    largest = limit if full else min(limit, max(-(-total // count), total * loads[0] // sum(loads)))
    least = 1 if total - largest >= count - 1 else 0
    holding, rest = [largest] + [least] * (count - 1), total - largest - least * (count - 1)
    while rest > 0:
        candidates = [i for i in range(1, count) if holding[i] < largest] or [i for i in range(1, count) if holding[i] < limit]
        whole, remaining = sum([loads[i] for i in candidates]), rest
        for i in candidates:
            extra = min(limit - holding[i], max(1, remaining * loads[i] // whole), rest)
            holding[i] = holding[i] + extra
            rest = rest - extra
    return np.array(holding)


def noise(own_key, dims, width, bound, cuts=(), kind=jnp.bfloat16):
    values = jax.random.normal(own_key, dims, jnp.float32) * width
    if len(cuts) > 0:
        values = shard_levels(own_key, dims, cuts, -0.22, 0.18) * values
    return jnp.clip(values, min=-bound, max=bound).astype(kind)


def setup_inputs(seed: int = 0) -> dict:
    key_list = jax.random.split(jax.random.key(seed), 12)
    queries = draw_queries(jax.random.fold_in(key_list[11], 71), 0)
    keys = draw_keys(jax.random.fold_in(key_list[11], 71), 0)
    values = noise(key_list[2], (SEQUENCE_TOKENS, KEY_VALUE_HEADS * HEAD_WIDTH), 8.0, 48.0, ((0, 32), (1, 4)))
    resid = noise(key_list[3], (SEQUENCE_TOKENS, D), 0.5, 3.0, ((0, 128),))
    out_weight = noise(key_list[4], (QUERY_HEADS * HEAD_WIDTH, D), (QUERY_HEADS * HEAD_WIDTH) ** -0.5, 0.0625, ((0, 4), (1, 32)))
    norm_gain = jnp.clip(1.0 + 0.18 * jax.random.normal(key_list[5], (D,), jnp.float32), 0.1, 1.9)
    routes_keys = jax.random.split(jax.random.fold_in(key_list[6], 1), SEQUENCE_TOKENS // TOK_OWN)
    routes_turns = jax.random.permutation(jax.random.fold_in(key_list[6], 3), SEQUENCE_TOKENS // TOK_OWN)
    routes = jax.vmap(lambda own, number: shared_out(jax.random.fold_in(key_list[6], 2), own, number, TOK_OWN, EXPERTS, TOPK, CAP, 2))(routes_keys, routes_turns).reshape((SEQUENCE_TOKENS, TOPK))
    gates = jnp.clip(0.05 + 0.29999999 * jax.random.uniform(key_list[7], (SEQUENCE_TOKENS, TOPK), jnp.float32) ** shard_levels(key_list[7], (SEQUENCE_TOKENS, TOPK), ((0, 128),), -0.2, 0.2), 0.05, 0.35)
    w_gate = noise(key_list[8], (EXPERTS, D, FF), D ** -0.5, 0.09375, ((0, 32), (2, 4)))
    w_up = noise(key_list[9], (EXPERTS, D, FF), D ** -0.5, 0.09375, ((0, 32), (2, 4)))
    w_down = noise(key_list[10], (EXPERTS, FF, D), FF ** -0.5, 0.15625, ((0, 32), (1, 4)))
    return dict(queries=queries, keys=keys, values=values, resid=resid, out_weight=out_weight, norm_gain=norm_gain, routes=routes, gates=gates, w_gate=w_gate, w_up=w_up, w_down=w_down)


def one_head(triple):
    query_head, key_head, value_head = triple
    scores = jnp.dot(query_head, key_head.T, preferred_element_type=jnp.float32) * HEAD_WIDTH ** (-0.5)
    places = jnp.arange(SEQUENCE_TOKENS, dtype=jnp.int32)
    keep = places[None, :] <= places[:, None]
    scores = jnp.where(keep, scores, -jnp.inf)
    highest = lax.optimization_barrier(jnp.max(scores, axis=1, keepdims=True))
    weights = jnp.exp(scores - highest)
    total = lax.optimization_barrier(jnp.sum(weights, axis=1, keepdims=True))
    summed = jnp.dot(weights.astype(jnp.bfloat16), value_head, preferred_element_type=jnp.float32)
    return (summed / total).astype(jnp.bfloat16)

def reference(queries, keys, values, resid, out_weight, norm_gain, routes, gates, w_gate, w_up, w_down):
    query_group = QUERY_HEADS // KEY_VALUE_HEADS
    query_heads = queries.reshape(SEQUENCE_TOKENS, QUERY_HEADS, HEAD_WIDTH).transpose(1, 0, 2)
    key_head_rows = jnp.repeat(keys.reshape(SEQUENCE_TOKENS, KEY_VALUE_HEADS, HEAD_WIDTH).transpose(1, 0, 2), query_group, axis=0)
    value_head_rows = jnp.repeat(values.reshape(SEQUENCE_TOKENS, KEY_VALUE_HEADS, HEAD_WIDTH).transpose(1, 0, 2), query_group, axis=0)
    attn = lax.map(one_head, (query_heads, key_head_rows, value_head_rows))
    attn = attn.transpose(1, 0, 2).reshape(SEQUENCE_TOKENS, QUERY_HEADS * HEAD_WIDTH)
    hsum = resid.astype(jnp.float32) + jnp.dot(attn, out_weight, preferred_element_type=jnp.float32)
    scale_rows = lax.rsqrt(lax.optimization_barrier(jnp.mean(hsum * hsum, axis=1, keepdims=True)) + 1e-06)
    normed = (hsum * scale_rows * norm_gain).astype(jnp.bfloat16)
    owners = SEQUENCE_TOKENS // TOK_OWN
    flat = routes.reshape(-1)
    per_block = flat.reshape(owners, TOK_OWN * TOPK)
    onehot = (per_block[:, :, None] == jnp.arange(EXPERTS, dtype=jnp.int32)[None, None, :]).astype(jnp.int32)
    before = jnp.cumsum(onehot, axis=1) - onehot
    slots = lax.optimization_barrier(jnp.sum(before * onehot, axis=2)).reshape(-1)
    owner_of = jnp.arange(SEQUENCE_TOKENS * TOPK, dtype=jnp.int32) // (TOK_OWN * TOPK)
    place = (owner_of * CAP + slots).astype(jnp.int32)
    source = jnp.repeat(normed, TOPK, axis=0)
    quarter = FF // N_TENSOR

    def expert_rows(inputs):
        index, gate_mat, up_mat, down_mat = inputs
        chosen = flat == index
        target = jnp.where(chosen, place, owners * CAP).astype(jnp.int32)
        buffer = jnp.zeros((owners * CAP, D), jnp.bfloat16).at[target].set(source, mode='drop')
        gating = jnp.dot(buffer, gate_mat, preferred_element_type=jnp.float32)
        upward = jnp.dot(buffer, up_mat, preferred_element_type=jnp.float32)
        hidden = (jax.nn.silu(gating) * upward).astype(jnp.bfloat16)
        summed = jnp.zeros((owners * CAP, D), jnp.float32)
        for block in range(N_TENSOR):
            piece = jnp.dot(hidden[:, block * quarter:(block + 1) * quarter], down_mat[block * quarter:(block + 1) * quarter, :], preferred_element_type=jnp.float32)
            piece = lax.optimization_barrier(piece.astype(jnp.bfloat16))
            summed = summed + piece.astype(jnp.float32)
        return summed.astype(jnp.bfloat16)
    outputs = lax.map(expert_rows, (jnp.arange(EXPERTS, dtype=jnp.int32), w_gate, w_up, w_down))
    picked = outputs[flat, place]
    contrib = jnp.einsum('tk,tkd->td', gates, picked.reshape(SEQUENCE_TOKENS, TOPK, D).astype(jnp.float32))
    return (hsum + contrib).astype(jnp.bfloat16)
```

```python
import functools
import jax
import jax.numpy as jnp
from jax import lax
from jax.experimental import pallas as pl
from jax.experimental.pallas import tpu as pltpu
from jax.sharding import PartitionSpec as P

D = 4096
HW = 128
MESH = pl.DeviceIdType.MESH
BF = jnp.bfloat16
F32 = jnp.float32


def place():
    c = lax.axis_index("context")
    t = lax.axis_index("tensor")
    return c // 8, (c // 2) % 4, c % 2, t // 2, t % 2


def device(z, x, yl, yh, core):
    return {"context": z * 8 + x * 2 + yl, "tensor": yh * 2 + core}


def send(src, dst, ssem, rsem, to):
    copy = pltpu.make_async_remote_copy(
        src_ref=src, dst_ref=dst, send_sem=ssem, recv_sem=rsem, device_id=to, device_id_type=MESH
    )
    copy.start()
    return copy


def greet(peers):
    barrier = pltpu.get_barrier_semaphore()
    for peer in peers:
        pl.semaphore_signal(barrier, inc=1, device_id=peer, device_id_type=MESH)
    pl.semaphore_wait(barrier, len(peers))


def attention_kernel(
    q_ref, k_ref, v_ref, w_ref, resid_ref, gain_ref, hsum_ref, normed_ref,
    kall, vall, wall, att, scores, acc, sib_out, sib_in, own_out, own_in,
    k_s, k_r, v_s, v_r, w_s, w_r, a_s, a_r, c_s, c_r, o_s, o_r,
):
    z, x, yl, yh, core = place()
    ctx = z * 8 + x * 2 + yl
    zs = [lax.rem(z + o, 4) for o in range(4)]
    xs = [lax.rem(x + o, 4) for o in range(4)]
    group = [(o, p) for o in range(4) for p in range(2)][1:]
    sibling = device(z, x, yl, yh, 1 - core)
    z_peers = [device(zs[o], x, yl, yh, core) for o in (1, 2, 3)]
    x_peers = [device(z, xs[o], yl, yh, core) for o in (1, 2, 3)]
    y_peer = device(z, x, 1 - yl, yh, core)
    w_peers = [device(z, xs[o], lax.rem(yl + p, 2), yh, core) for o, p in group]
    o_peers = [device(zs[o], x, yl, lax.rem(yh + p, 2), core) for o, p in group]
    greet([sibling] + z_peers + w_peers + [device(zs[o], x, yl, 1 - yh, core) for o in range(4)])

    kall[z, x, yl] = k_ref[...]
    vall[z, x, yl] = v_ref[...]
    me = (z, x, yl)
    k1 = [send(kall.at[me], kall.at[me], k_s.at[i], k_r.at[i], z_peers[i]) for i in range(3)]
    v1 = [send(vall.at[me], vall.at[me], v_s.at[0], v_r.at[0], y_peer)]
    for copy in v1 + k1:
        copy.wait_recv()
    k2 = [
        send(kall.at[:, x, yl], kall.at[:, x, yl], k_s.at[3 + i], k_r.at[3 + i], x_peers[i])
        for i in range(3)
    ]
    v2 = [
        send(vall.at[z, x], vall.at[z, x], v_s.at[1 + i], v_r.at[1 + i], x_peers[i])
        for i in range(3)
    ]
    for copy in v2 + k2:
        copy.wait_recv()
    k3 = [send(kall.at[:, :, yl], kall.at[:, :, yl], k_s.at[6], k_r.at[6], y_peer)]
    v3 = [send(vall.at[z], vall.at[z], v_s.at[4 + i], v_r.at[4 + i], z_peers[i]) for i in range(3)]
    mine = pl.ds(pl.multiple_of((x * 2 + yl) * 128, 128), 128)
    wcopies = [
        send(w_ref, wall.at[:, mine], w_s.at[i], w_r.at[i], w_peers[i]) for i in range(7)
    ]
    wall[:, mine] = w_ref[...]
    for copy in v3 + k3:
        copy.wait_recv()

    factor = HW**-0.5 * 1.4426950408889634
    last = ctx // 4
    nrow = 512

    def keys_of(ref, ch):
        return ref[ch // 2, pl.ds((ch % 2) * 2, 2)].reshape(512, HW)

    def columns(ch):
        return pl.ds(pl.multiple_of(ch * 512, 512), 512)

    def fold(f, s):
        return f(f(s[:, 0:128], s[:, 128:256]), f(s[:, 256:384], s[:, 384:512]))

    def heads(hc, carry):
        q = jnp.concatenate(
            [
                q_ref[:, pl.ds(pl.multiple_of(hc * 512 + i * HW, HW), HW)]
                for i in range(4)
            ],
            axis=0,
        )

        def product(ch):
            return lax.dot_general(
                q, keys_of(kall, ch), (((1,), (1,)), ((), ())), preferred_element_type=F32
            )

        def first(ch, top):
            s = product(ch)
            scores[:, columns(ch)] = s
            return jnp.maximum(top, fold(jnp.maximum, s))

        top = lax.fori_loop(0, last, first, jnp.full((nrow, 128), -jnp.inf, F32))
        s = product(last)
        row = lax.broadcasted_iota(jnp.int32, (nrow, 512), 0) % 128
        col = lax.broadcasted_iota(jnp.int32, (nrow, 512), 1)
        s = jnp.where(col <= row + (ctx % 4) * 128, s, -jnp.inf)
        scores[:, columns(last)] = s
        top = jnp.maximum(top, fold(jnp.maximum, s))
        shift = jnp.max(top, axis=1, keepdims=True) * factor

        def second(ch, carry):
            total, summed = carry
            p = jnp.exp2(scores[:, columns(ch)] * factor - shift)
            total = total + fold(jnp.add, p)
            summed = summed + jnp.dot(p.astype(BF), keys_of(vall, ch), preferred_element_type=F32)
            return total, summed

        zero = jnp.zeros((nrow, 128), F32)
        total, summed = lax.fori_loop(0, last + 1, second, (zero, zero))
        out = (summed / jnp.sum(total, axis=1, keepdims=True)).astype(BF)
        for i in range(4):
            att[z, hc, :, i * HW : (i + 1) * HW] = out[i * 128 : (i + 1) * 128]
        for i in range(3):
            send(att.at[z, hc], att.at[z, hc], a_s.at[hc, i], a_r.at[hc, i], z_peers[i])
        return carry

    lax.fori_loop(0, 4, heads, 0)
    for copy in wcopies:
        copy.wait_recv()

    def project(hc, carry):
        for i in range(3):
            pltpu.make_async_remote_copy(
                src_ref=att.at[z, hc], dst_ref=att.at[z, hc], send_sem=a_s.at[hc, i],
                recv_sem=a_r.at[hc, i], device_id=z_peers[i], device_id_type=MESH,
            ).wait()
        a = att[:, hc].reshape(512, 512)
        for n in range(4):
            cols = slice(n * 256, (n + 1) * 256)
            r = jnp.dot(
                a, wall[pl.ds(pl.multiple_of(hc * 512, 512), 512), cols], preferred_element_type=F32
            ).reshape(4, 2, 2, 32, 256)
            acc[:, :, :, :, cols] = jnp.where(hc == 0, r, acc[:, :, :, :, cols] + r)
        return carry

    acc[...] = jnp.zeros_like(acc)
    lax.fori_loop(0, 4, project, 0)
    sib_out[...] = acc[:, :, 1 - core].astype(BF)
    copy = send(sib_out, sib_in, c_s.at[0], c_r.at[0], sibling)
    copy.wait()
    own_out[...] = (acc[:, :, core] + sib_in[...].astype(F32)).astype(BF)
    ocopies = []
    for i, (o, p) in enumerate(group):
        ocopies.append(
            send(
                own_out.at[zs[o], lax.rem(yh + p, 2)], own_in.at[z, yh], o_s.at[i], o_r.at[i], o_peers[i]
            )
        )
    own_in[z, yh] = own_out[z, yh]
    for copy in ocopies:
        copy.wait()
    square = jnp.zeros((32, 1), F32)
    for n in range(4):
        h = resid_ref[:, n * 1024 : (n + 1) * 1024].astype(F32) + (
            own_in[n, 0].astype(F32) + own_in[n, 1].astype(F32)
        )
        hsum_ref[n] = h
        square = square + jnp.sum(h * h, axis=1, keepdims=True)
    scale = lax.rsqrt(square * (1.0 / D) + 1e-06)
    for n in range(4):
        normed_ref[n] = (hsum_ref[n] * scale * gain_ref[:, n * 1024 : (n + 1) * 1024]).astype(BF)
    for copy in k1 + k2 + k3 + v1 + v2 + v3 + wcopies:
        copy.wait_send()


def attention(queries, keys, values, out_weight, resid, norm_gain):
    dma = pltpu.SemaphoreType.DMA
    vm = pl.BlockSpec(memory_space=pltpu.VMEM)
    return pl.pallas_call(
        attention_kernel,
        out_shape=(
            jax.ShapeDtypeStruct((4, 32, 1024), F32),
            jax.ShapeDtypeStruct((4, 32, 1024), BF),
        ),
        in_specs=[vm] * 6,
        out_specs=(vm, vm),
        scratch_shapes=[
            pltpu.VMEM((4, 4, 2, 128, 128), BF),
            pltpu.VMEM((4, 4, 2, 128, 128), BF),
            pltpu.VMEM((2048, 1024), BF),
            pltpu.VMEM((4, 4, 128, 512), BF),
            pltpu.VMEM((512, 4096), F32),
            pltpu.VMEM((4, 2, 2, 32, 1024), F32),
            pltpu.VMEM((4, 2, 32, 1024), BF),
            pltpu.VMEM((4, 2, 32, 1024), BF),
            pltpu.VMEM((4, 2, 32, 1024), BF),
            pltpu.VMEM((4, 2, 32, 1024), BF),
            dma((7,)), dma((7,)), dma((7,)), dma((7,)), dma((7,)), dma((7,)),
            dma((4, 3)), dma((4, 3)), dma((1,)), dma((1,)), dma((7,)), dma((7,)),
        ],
        compiler_params=pltpu.CompilerParams(
            collective_id=0, has_side_effects=True, vmem_limit_bytes=56 * 2**20
        ),
        cost_estimate=pl.CostEstimate(flops=8 * 10**9, bytes_accessed=4 * 2**20, transcendentals=8 * 2**20),
    )(queries, keys, values, out_weight, resid, norm_gain.reshape(1, D))


EXP_DEV = 2


def shards(
    queries, keys, values, resid, out_weight, norm_gain, routes, gates, w_gate, w_up, w_down
):
    n_ctx = lax.axis_size("context")
    hsum, normed = attention(queries, keys, values, out_weight, resid, norm_gain)
    hsum = hsum.transpose(1, 0, 2).reshape(32, D)
    normed = normed.transpose(1, 0, 2).reshape(32, D)
    tok_own = resid.shape[0]
    topk = routes.shape[1]
    experts = EXP_DEV * n_ctx
    capacity = max(2, 3 * tok_own * topk // (2 * experts))
    flat = routes.reshape(-1)
    onehot = (flat[:, None] == jnp.arange(experts, dtype=jnp.int32)[None, :]).astype(jnp.int32)
    slots = jnp.sum((jnp.cumsum(onehot, axis=0) - onehot) * onehot, axis=1)
    place = flat * capacity + slots
    outgoing = (
        jnp.zeros((experts * capacity, D), jnp.bfloat16)
        .at[place]
        .set(jnp.repeat(normed, topk, axis=0))
    )
    outgoing = outgoing.reshape(n_ctx, EXP_DEV, capacity, D)
    arrived = lax.all_to_all(outgoing, "context", split_axis=0, concat_axis=0, tiled=True)
    shared = lax.all_gather(arrived, "tensor", axis=0, tiled=True)
    gating = jnp.einsum("sjcd,jdf->sjcf", shared, w_gate, preferred_element_type=jnp.float32)
    upward = jnp.einsum("sjcd,jdf->sjcf", shared, w_up, preferred_element_type=jnp.float32)
    hidden = (jax.nn.silu(gating) * upward).astype(jnp.bfloat16)
    reduced = lax.psum_scatter(
        jnp.einsum("sjcf,jfd->sjcd", hidden, w_down, preferred_element_type=jnp.float32).astype(
            jnp.bfloat16
        ),
        "tensor",
        scatter_dimension=0,
        tiled=True,
    )
    results = lax.all_to_all(reduced, "context", split_axis=0, concat_axis=0, tiled=True)
    picked = results.reshape(experts * capacity, D)[place]
    contrib = jnp.einsum("tk,tkd->td", gates, picked.reshape(tok_own, topk, D).astype(jnp.float32))
    return (hsum + contrib).astype(jnp.bfloat16)


def solution(mesh):
    return jax.shard_map(
        shards,
        mesh=mesh,
        in_specs=(
            P("context", "tensor"),
            P("context", "tensor"),
            P("context", "tensor"),
            P(("context", "tensor"), None),
            P("tensor", "context"),
            P(),
            P(("context", "tensor"), None),
            P(("context", "tensor"), None),
            P("context", None, "tensor"),
            P("context", None, "tensor"),
            P("context", "tensor", None),
        ),
        out_specs=P(("context", "tensor"), None),
        check_vma=False,
    )
```

```python
import functools
import jax
import jax.numpy as jnp
from jax import lax
from jax.experimental import pallas as pl
from jax.experimental.pallas import tpu as pltpu
from jax.sharding import PartitionSpec as P

D = 4096
HW = 128
MESH = pl.DeviceIdType.MESH
BF = jnp.bfloat16
F32 = jnp.float32


def place():
    c = lax.axis_index("context")
    t = lax.axis_index("tensor")
    return c // 8, (c // 2) % 4, c % 2, t // 2, t % 2


def device(z, x, yl, yh, core):
    return {"context": z * 8 + x * 2 + yl, "tensor": yh * 2 + core}


def send(src, dst, ssem, rsem, to):
    copy = pltpu.make_async_remote_copy(
        src_ref=src, dst_ref=dst, send_sem=ssem, recv_sem=rsem, device_id=to, device_id_type=MESH
    )
    copy.start()
    return copy


def greet(peers):
    barrier = pltpu.get_barrier_semaphore()
    for peer in peers:
        pl.semaphore_signal(barrier, inc=1, device_id=peer, device_id_type=MESH)
    pl.semaphore_wait(barrier, len(peers))


def attention_kernel(
    q_ref, k_ref, v_ref, w_ref, resid_ref, gain_ref, hsum_ref, normed_ref,
    kall, vall, wall, att, scores, acc, sib_out, sib_in, own_out, own_in,
    k_s, k_r, v_s, v_r, w_s, w_r, a_s, a_r, c_s, c_r, o_s, o_r,
):
    z, x, yl, yh, core = place()
    ctx = z * 8 + x * 2 + yl
    zs = [lax.rem(z + o, 4) for o in range(4)]
    xs = [lax.rem(x + o, 4) for o in range(4)]
    group = [(o, p) for o in range(4) for p in range(2)][1:]
    sibling = device(z, x, yl, yh, 1 - core)
    z_peers = [device(zs[o], x, yl, yh, core) for o in (1, 2, 3)]
    x_peers = [device(z, xs[o], yl, yh, core) for o in (1, 2, 3)]
    y_peer = device(z, x, 1 - yl, yh, core)
    w_peers = [device(z, xs[o], lax.rem(yl + p, 2), yh, core) for o, p in group]
    o_peers = [device(zs[o], x, yl, lax.rem(yh + p, 2), core) for o, p in group]
    greet([sibling] + z_peers + w_peers + [device(zs[o], x, yl, 1 - yh, core) for o in range(4)])

    kall[z, x, yl] = k_ref[...]
    vall[z, x, yl] = v_ref[...]
    me = (z, x, yl)
    k1 = [send(kall.at[me], kall.at[me], k_s.at[i], k_r.at[i], z_peers[i]) for i in range(3)]
    v1 = [send(vall.at[me], vall.at[me], v_s.at[0], v_r.at[0], y_peer)]
    for copy in v1 + k1:
        copy.wait_recv()
    k2 = [
        send(kall.at[:, x, yl], kall.at[:, x, yl], k_s.at[3 + i], k_r.at[3 + i], x_peers[i])
        for i in range(3)
    ]
    v2 = [
        send(vall.at[z, x], vall.at[z, x], v_s.at[1 + i], v_r.at[1 + i], x_peers[i])
        for i in range(3)
    ]
    for copy in v2 + k2:
        copy.wait_recv()
    k3 = [send(kall.at[:, :, yl], kall.at[:, :, yl], k_s.at[6], k_r.at[6], y_peer)]
    v3 = [send(vall.at[z], vall.at[z], v_s.at[4 + i], v_r.at[4 + i], z_peers[i]) for i in range(3)]
    mine = pl.ds(pl.multiple_of((x * 2 + yl) * 128, 128), 128)
    wcopies = [
        send(w_ref, wall.at[:, mine], w_s.at[i], w_r.at[i], w_peers[i]) for i in range(7)
    ]
    wall[:, mine] = w_ref[...]
    for copy in v3 + k3:
        copy.wait_recv()

    factor = HW**-0.5 * 1.4426950408889634
    last = ctx // 4
    nrow = 512

    def keys_of(ref, ch):
        return ref[ch // 2, pl.ds((ch % 2) * 2, 2)].reshape(512, HW)

    def columns(ch):
        return pl.ds(pl.multiple_of(ch * 512, 512), 512)

    def fold(f, s):
        return f(f(s[:, 0:128], s[:, 128:256]), f(s[:, 256:384], s[:, 384:512]))

    def heads(hc, carry):
        q = jnp.concatenate(
            [
                q_ref[:, pl.ds(pl.multiple_of(hc * 512 + i * HW, HW), HW)]
                for i in range(4)
            ],
            axis=0,
        )

        def product(ch):
            return lax.dot_general(
                q, keys_of(kall, ch), (((1,), (1,)), ((), ())), preferred_element_type=F32
            )

        def first(ch, top):
            s = product(ch)
            scores[:, columns(ch)] = s
            return jnp.maximum(top, fold(jnp.maximum, s))

        top = lax.fori_loop(0, last, first, jnp.full((nrow, 128), -jnp.inf, F32))
        s = product(last)
        row = lax.broadcasted_iota(jnp.int32, (nrow, 512), 0) % 128
        col = lax.broadcasted_iota(jnp.int32, (nrow, 512), 1)
        s = jnp.where(col <= row + (ctx % 4) * 128, s, -jnp.inf)
        scores[:, columns(last)] = s
        top = jnp.maximum(top, fold(jnp.maximum, s))
        shift = jnp.max(top, axis=1, keepdims=True) * factor

        def second(ch, carry):
            total, summed = carry
            p = jnp.exp2(scores[:, columns(ch)] * factor - shift)
            total = total + fold(jnp.add, p)
            summed = summed + jnp.dot(p.astype(BF), keys_of(vall, ch), preferred_element_type=F32)
            return total, summed

        zero = jnp.zeros((nrow, 128), F32)
        total, summed = lax.fori_loop(0, last + 1, second, (zero, zero))
        out = (summed / jnp.sum(total, axis=1, keepdims=True)).astype(BF)
        for i in range(4):
            att[z, hc, :, i * HW : (i + 1) * HW] = out[i * 128 : (i + 1) * 128]
        for i in range(3):
            send(att.at[z, hc], att.at[z, hc], a_s.at[hc, i], a_r.at[hc, i], z_peers[i])
        return carry

    lax.fori_loop(0, 4, heads, 0)
    for copy in wcopies:
        copy.wait_recv()

    def project(hc, carry):
        for i in range(3):
            pltpu.make_async_remote_copy(
                src_ref=att.at[z, hc], dst_ref=att.at[z, hc], send_sem=a_s.at[hc, i],
                recv_sem=a_r.at[hc, i], device_id=z_peers[i], device_id_type=MESH,
            ).wait()
        a = att[:, hc].reshape(512, 512)
        for n in range(4):
            cols = slice(n * 256, (n + 1) * 256)
            r = jnp.dot(
                a, wall[pl.ds(pl.multiple_of(hc * 512, 512), 512), cols], preferred_element_type=F32
            ).reshape(4, 2, 2, 32, 256)
            acc[:, :, :, :, cols] = jnp.where(hc == 0, r, acc[:, :, :, :, cols] + r)
        return carry

    acc[...] = jnp.zeros_like(acc)
    lax.fori_loop(0, 4, project, 0)
    sib_out[...] = acc[:, :, 1 - core].astype(BF)
    copy = send(sib_out, sib_in, c_s.at[0], c_r.at[0], sibling)
    copy.wait()
    own_out[...] = (acc[:, :, core] + sib_in[...].astype(F32)).astype(BF)
    ocopies = []
    for i, (o, p) in enumerate(group):
        ocopies.append(
            send(
                own_out.at[zs[o], lax.rem(yh + p, 2)], own_in.at[z, yh], o_s.at[i], o_r.at[i], o_peers[i]
            )
        )
    own_in[z, yh] = own_out[z, yh]
    for copy in ocopies:
        copy.wait()
    square = jnp.zeros((32, 1), F32)
    for n in range(4):
        h = resid_ref[:, n * 1024 : (n + 1) * 1024].astype(F32) + (
            own_in[n, 0].astype(F32) + own_in[n, 1].astype(F32)
        )
        hsum_ref[n] = h
        square = square + jnp.sum(h * h, axis=1, keepdims=True)
    scale = lax.rsqrt(square * (1.0 / D) + 1e-06)
    for n in range(4):
        normed_ref[n] = (hsum_ref[n] * scale * gain_ref[:, n * 1024 : (n + 1) * 1024]).astype(BF)
    for copy in k1 + k2 + k3 + v1 + v2 + v3 + wcopies:
        copy.wait_send()


def attention(queries, keys, values, out_weight, resid, norm_gain):
    dma = pltpu.SemaphoreType.DMA
    vm = pl.BlockSpec(memory_space=pltpu.VMEM)
    return pl.pallas_call(
        attention_kernel,
        out_shape=(
            jax.ShapeDtypeStruct((4, 32, 1024), F32),
            jax.ShapeDtypeStruct((4, 32, 1024), BF),
        ),
        in_specs=[vm] * 6,
        out_specs=(vm, vm),
        scratch_shapes=[
            pltpu.VMEM((4, 4, 2, 128, 128), BF),
            pltpu.VMEM((4, 4, 2, 128, 128), BF),
            pltpu.VMEM((2048, 1024), BF),
            pltpu.VMEM((4, 4, 128, 512), BF),
            pltpu.VMEM((512, 4096), F32),
            pltpu.VMEM((4, 2, 2, 32, 1024), F32),
            pltpu.VMEM((4, 2, 32, 1024), BF),
            pltpu.VMEM((4, 2, 32, 1024), BF),
            pltpu.VMEM((4, 2, 32, 1024), BF),
            pltpu.VMEM((4, 2, 32, 1024), BF),
            dma((7,)), dma((7,)), dma((7,)), dma((7,)), dma((7,)), dma((7,)),
            dma((4, 3)), dma((4, 3)), dma((1,)), dma((1,)), dma((7,)), dma((7,)),
        ],
        compiler_params=pltpu.CompilerParams(
            collective_id=0, has_side_effects=True, vmem_limit_bytes=56 * 2**20
        ),
        cost_estimate=pl.CostEstimate(flops=8 * 10**9, bytes_accessed=4 * 2**20, transcendentals=8 * 2**20),
    )(queries, keys, values, out_weight, resid, norm_gain.reshape(1, D))


CH = 4
CW = D // CH


def experts_kernel(
    normed_ref, hsum_ref, routes_ref, gates_ref, wg_ref, wu_ref, wd_ref, out_ref,
    tok, meta, stage, rows, acc, hid, wgu, wdn, back, zin, uin, vout, vin, pick, give,
    m_s, m_r, s1_s, s1_r, s2_s, s2_r, s3_s, s3_r, s4_s, s4_r,
    y_s, y_r, b3_s, b3_r, b2_s, b2_r, b1_s, b1_r, wg_m, wu_m, wd_m,
):
    z, x, yl, yh, core = place()
    y = yh * 2 + yl
    a = z * (1 - core) + x * core
    c = x * (1 - core) + z * core

    def at(a_, y_, c_):
        return device(
            a_ * (1 - core) + c_ * core, c_ * (1 - core) + a_ * core, y_ % 2, y_ // 2, core
        )

    As = [lax.rem(a + o, 4) for o in range(4)]
    Ys = [lax.rem(y + o, 4) for o in range(4)]
    Cs = [lax.rem(c + o, 4) for o in range(4)]
    a_peers = [at(As[o], y, c) for o in (1, 2, 3)]
    y_peers = [at(a, Ys[o], c) for o in (1, 2, 3)]
    c_peers = [at(a, y, Cs[o]) for o in (1, 2, 3)]
    sibling = device(z, x, yl, yh, 1 - core)
    greet([sibling] + a_peers + y_peers + c_peers)

    def remote(src, dst, ssem, rsem, to):
        return pltpu.make_async_remote_copy(
            src_ref=src, dst_ref=dst, send_sem=ssem, recv_sem=rsem, device_id=to, device_id_type=MESH
        )

    def m1(i):
        return remote(meta.at[y, a], meta.at[y, a], m_s.at[i], m_r.at[i], a_peers[i])

    def m2(i):
        return remote(meta.at[y], meta.at[y], m_s.at[3 + i], m_r.at[3 + i], y_peers[i])

    def s1(q, i):
        return remote(normed_ref.at[q], tok.at[q, y, a], s1_s.at[q, i], s1_r.at[q, i], a_peers[i])

    def s2(q, i):
        return remote(tok.at[q, y], tok.at[q, y], s2_s.at[q, i], s2_r.at[q, i], y_peers[i])

    def s3(q, i):
        return remote(
            stage.at[q, i], rows.at[q, 0, :, c], s3_s.at[q, i], s3_r.at[q, i], c_peers[i]
        )

    def s4(q):
        return remote(rows.at[q, 0], rows.at[q, 1], s4_s.at[q], s4_r.at[q], sibling)

    def yb(q):
        return remote(rows.at[q, 1], back.at[q], y_s.at[q], y_r.at[q], sibling)

    def b3(q, i):
        return remote(
            rows.at[q, 0, :, Cs[i + 1]], zin.at[q, c], b3_s.at[q, i], b3_r.at[q, i], c_peers[i]
        )

    def b2(q, i):
        return remote(tok.at[q, Ys[i + 1]], uin.at[q, y], b2_s.at[q, i], b2_r.at[q, i], y_peers[i])

    def b1(q, i):
        return remote(vout.at[q, As[i + 1]], vin.at[q, a], b1_s.at[q, i], b1_r.at[q, i], a_peers[i])

    def load_up(q):
        slot = q % 2
        depth = pl.ds(pl.multiple_of(q * CW, CW), CW)
        return (
            pltpu.make_async_copy(wg_ref.at[:, depth], wgu.at[slot, :, :, 0:384], wg_m.at[slot]),
            pltpu.make_async_copy(wu_ref.at[:, depth], wgu.at[slot, :, :, 384:768], wu_m.at[slot]),
        )

    def load_down(q):
        return pltpu.make_async_copy(
            wd_ref.at[:, :, q * CW : (q + 1) * CW], wdn.at[q % 3], wd_m.at[q]
        )

    lane = lax.broadcasted_iota(jnp.int32, (32, 128), 1)
    named = jnp.zeros((32, 128), F32)
    gate = jnp.zeros((32, 128), F32)
    for k in range(8):
        hit = routes_ref[:, k : k + 1] == lane % 64
        named = named + jnp.where(hit, 1.0, 0.0)
        gate = gate + jnp.where(hit, gates_ref[:, k : k + 1], 0.0)
    before = (
        lax.broadcasted_iota(jnp.int32, (32, 32), 1) < lax.broadcasted_iota(jnp.int32, (32, 32), 0)
    )
    rank = jnp.dot(
        jnp.where(before, 1.0, 0.0).astype(BF), named.astype(BF), preferred_element_type=F32
    )
    meta[y, a] = jnp.where(lane < 64, jnp.where(named > 0.5, rank, -1.0), gate).astype(BF)
    for i in range(3):
        m1(i).start()

    def first(q, carry):
        tok[q, y, a] = normed_ref[q]
        for i in range(3):
            s1(q, i).start()
        return carry

    lax.fori_loop(0, CH, first, 0)
    for q in range(2):
        for copy in load_up(q):
            copy.start()
    for q in range(3):
        load_down(q).start()
    for i in range(3):
        m1(i).wait()
    for i in range(3):
        m2(i).start()

    def second(q, carry):
        for i in range(3):
            s1(q, i).wait()
        for i in range(3):
            s2(q, i).start()
        return carry

    lax.fori_loop(0, CH, second, 0)
    for i in range(3):
        m2(i).wait()

    info = meta[...].reshape(512, 128)
    base = a * (16 * (1 - core) + 4 * core) + 2 * yl
    step_c = 4 * (1 - core) + 16 * core
    m_lane = lax.broadcasted_iota(jnp.int32, (128, 128), 1)
    l_row = lax.broadcasted_iota(jnp.int32, (128, 128), 0)
    want = base + (m_lane // 2) * step_c + m_lane % 2
    pick_rank = jnp.where((l_row == want) & (m_lane < 8), 1.0, 0.0).astype(BF)
    pick_gate = jnp.where((l_row == want + 64) & (m_lane < 8), 1.0, 0.0).astype(BF)
    rank_col = jnp.dot(info, pick_rank, preferred_element_type=F32)
    gate_col = jnp.dot(info, pick_gate, preferred_element_type=F32)
    m_row = lax.broadcasted_iota(jnp.int32, (16, 128), 0)
    l_lane = lax.broadcasted_iota(jnp.int32, (16, 128), 1)
    pick_row = jnp.where(
        l_lane == base + (m_row // 2) * step_c + m_row % 2, 1.0, 0.0
    ).astype(BF)
    rank_row = lax.dot_general(
        pick_row, info, (((1,), (1,)), ((), ())), preferred_element_type=F32
    )
    src_row = (lax.broadcasted_iota(jnp.int32, (16, 512), 1) // 32).astype(F32)
    code_row = jnp.where(rank_row > -0.5, src_row * 6.0 + rank_row, -1.0)
    src_col = (lax.broadcasted_iota(jnp.int32, (512, 128), 0) // 32).astype(F32)
    code_col = jnp.where(rank_col > -0.5, src_col * 6.0 + rank_col, -1000.0)
    at_row = lax.broadcasted_iota(jnp.int32, (96, 512), 0).astype(F32)
    at_col = lax.broadcasted_iota(jnp.int32, (512, 768), 1).astype(F32)
    weight = jnp.zeros((512, 768), F32)
    for m in range(8):
        pick[m // 2, (m % 2) * 96 : (m % 2 + 1) * 96] = jnp.where(
            at_row == code_row[m : m + 1], 1.0, 0.0
        ).astype(BF)
        weight = weight + jnp.where(
            at_col == code_col[:, m : m + 1] + (96.0 * m), gate_col[:, m : m + 1], 0.0
        )
    give[...] = weight.astype(BF)

    def select(q):
        for i in range(3):
            s2(q, i).wait_recv()

        def one(o):
            p = pick[lax.rem(c + o, 4)]
            parts = [
                jnp.dot(
                    p,
                    tok[q, :, :, :, n * 256 : (n + 1) * 256].reshape(512, 256),
                    preferred_element_type=F32,
                ).astype(BF).reshape(2, 96, 256)
                for n in range(CW // 256)
            ]
            return parts

        def other(i, carry):
            for n, part in enumerate(one(i + 1)):
                stage[q, i, :, :, n * 256 : (n + 1) * 256] = part
            return carry

        lax.fori_loop(0, 3, other, 0)
        for i in range(3):
            s3(q, i).start()
        for n, part in enumerate(one(0)):
            rows[q, 0, :, c, :, n * 256 : (n + 1) * 256] = part

    def share(q):
        for i in range(3):
            s3(q, i).wait_recv()
        s4(q).start()

    def up(q):
        for copy in load_up(q):
            copy.wait()
        s4(q).wait_recv()
        slot = q % 2

        def one(i, carry):
            s, j = i // 2, i % 2
            r = rows[q, s, j].reshape(384, CW)
            for n in range(3):
                cols = slice(n * 256, (n + 1) * 256)
                d = jnp.dot(r, wgu[slot, j, :, cols], preferred_element_type=F32)
                acc[s, j, :, cols] = acc[s, j, :, cols] + d
            return carry

        lax.fori_loop(0, 4, one, 0)

        @pl.when(q < CH - 2)
        def _():
            for copy in load_up(q + 2):
                copy.start()

    acc[...] = jnp.zeros_like(acc)

    def dispatch(step, carry):
        @pl.when(step < CH)
        def _():
            select(step)

        @pl.when((step >= 1) & (step < CH + 1))
        def _():
            share(step - 1)

        @pl.when(step >= 2)
        def _():
            up(step - 2)

        return carry

    lax.fori_loop(0, CH + 2, dispatch, 0)

    def activate(i, carry):
        s, j = i // 2, i % 2
        v = acc[s, j, :, 0:384]
        hid[s, j] = (v / (1.0 + jnp.exp(-v)) * acc[s, j, :, 384:768]).astype(BF)
        return carry

    lax.fori_loop(0, 4, activate, 0)
    for q in range(3):
        load_down(q).wait()

    def down(q, s, j, n):
        return jnp.dot(
            hid[s, j], wdn[lax.rem(q, 3), j, :, n * 256 : (n + 1) * 256], preferred_element_type=F32
        )

    def half(step, carry):
        @pl.when(step < CH)
        def _():
            def one(j, carry):
                for n in range(CW // 256):
                    rows[step, 1, j, :, :, n * 256 : (n + 1) * 256] = (
                        down(step, 1, j, n).astype(BF).reshape(4, 96, 256)
                    )
                return carry

            lax.fori_loop(0, 2, one, 0)
            yb(step).start()

        @pl.when(step >= 1)
        def _():
            q = step - 1
            s4(q).wait_send()
            yb(q).wait_recv()

            def one(j, carry):
                for n in range(CW // 256):
                    cols = slice(n * 256, (n + 1) * 256)
                    v = down(q, 0, j, n).reshape(4, 96, 256) + back[q, j, :, :, cols].astype(F32)
                    rows[q, 0, j, :, :, cols] = v.astype(BF)
                return carry

            lax.fori_loop(0, 2, one, 0)
            for i in range(3):
                b3(q, i).start()
            zin[q, c] = rows[q, 0, :, c]

            @pl.when(q == 0)
            def _():
                load_down(3).start()

            @pl.when(q == 1)
            def _():
                load_down(3).wait()

        return carry

    lax.fori_loop(0, CH + 1, half, 0)

    def combine(step, carry):
        @pl.when(step < CH)
        def _():
            q = step
            for i in range(3):
                b3(q, i).wait_recv()
            for i in range(3):
                s2(q, i).wait_send()

            def one(y_):
                g = give[pl.ds(pl.multiple_of(y_ * 128, 128), 128)]
                return [
                    jnp.dot(
                        g,
                        zin[q, :, :, :, n * 256 : (n + 1) * 256].reshape(768, 256),
                        preferred_element_type=F32,
                    ).astype(BF).reshape(4, 32, 256)
                    for n in range(CW // 256)
                ]

            def other(i, carry):
                y_ = lax.rem(y + i + 1, 4)
                for n, part in enumerate(one(y_)):
                    tok[q, y_, :, :, n * 256 : (n + 1) * 256] = part
                return carry

            lax.fori_loop(0, 3, other, 0)
            for i in range(3):
                b2(q, i).start()
            for n, part in enumerate(one(y)):
                uin[q, y, :, :, n * 256 : (n + 1) * 256] = part

        @pl.when((step >= 1) & (step < CH + 1))
        def _():
            q = step - 1
            for i in range(3):
                b2(q, i).wait_recv()
            v = uin[q, 0].astype(F32) + uin[q, 1].astype(F32)
            v = v + uin[q, 2].astype(F32) + uin[q, 3].astype(F32)
            vout[q] = v.astype(BF)
            for i in range(3):
                b1(q, i).start()
            vin[q, a] = vout[q, a]

        @pl.when(step >= 2)
        def _():
            q = step - 2
            for i in range(3):
                b1(q, i).wait_recv()
            v = vin[q, 0].astype(F32) + vin[q, 1].astype(F32)
            v = v + vin[q, 2].astype(F32) + vin[q, 3].astype(F32)
            out_ref[:, pl.ds(pl.multiple_of(q * CW, CW), CW)] = (hsum_ref[q] + v).astype(BF)

        return carry

    lax.fori_loop(0, CH + 2, combine, 0)

    def finish(q, carry):
        yb(q).wait_send()
        for i in range(3):
            s3(q, i).wait_send()
            b3(q, i).wait_send()
            b2(q, i).wait_send()
            b1(q, i).wait_send()
        return carry

    lax.fori_loop(0, CH, finish, 0)


def mixture(normed, hsum, routes, gates, w_gate, w_up, w_down):
    dma = pltpu.SemaphoreType.DMA
    vm = pl.BlockSpec(memory_space=pltpu.VMEM)
    hbm = pl.BlockSpec(memory_space=pl.ANY)
    return pl.pallas_call(
        experts_kernel,
        out_shape=jax.ShapeDtypeStruct((32, D), BF),
        in_specs=[vm] * 4 + [hbm] * 3,
        out_specs=vm,
        scratch_shapes=[
            pltpu.VMEM((CH, 4, 4, 32, CW), BF),
            pltpu.VMEM((4, 4, 32, 128), BF),
            pltpu.VMEM((CH, 3, 2, 96, CW), BF),
            pltpu.VMEM((CH, 2, 2, 4, 96, CW), BF),
            pltpu.VMEM((2, 2, 384, 768), F32),
            pltpu.VMEM((2, 2, 384, 384), BF),
            pltpu.VMEM((2, 2, CW, 768), BF),
            pltpu.VMEM((3, 2, 384, CW), BF),
            pltpu.VMEM((CH, 2, 4, 96, CW), BF),
            pltpu.VMEM((CH, 4, 2, 96, CW), BF),
            pltpu.VMEM((CH, 4, 4, 32, CW), BF),
            pltpu.VMEM((CH, 4, 32, CW), BF),
            pltpu.VMEM((CH, 4, 32, CW), BF),
            pltpu.VMEM((4, 192, 512), BF),
            pltpu.VMEM((512, 768), BF),
            dma((6,)), dma((6,)),
            dma((CH, 3)), dma((CH, 3)), dma((CH, 3)), dma((CH, 3)), dma((CH, 3)), dma((CH, 3)),
            dma((CH,)), dma((CH,)), dma((CH,)), dma((CH,)),
            dma((CH, 3)), dma((CH, 3)), dma((CH, 3)), dma((CH, 3)), dma((CH, 3)), dma((CH, 3)),
            dma((2,)), dma((2,)), dma((CH,)),
        ],
        compiler_params=pltpu.CompilerParams(
            collective_id=1, has_side_effects=True, vmem_limit_bytes=63 * 2**20
        ),
        cost_estimate=pl.CostEstimate(
            flops=20 * 10**9, bytes_accessed=20 * 2**20, transcendentals=2**20
        ),
    )(normed, hsum, routes, gates, w_gate, w_up, w_down)


def shards(
    queries, keys, values, resid, out_weight, norm_gain, routes, gates, w_gate, w_up, w_down
):
    hsum, normed = attention(queries, keys, values, out_weight, resid, norm_gain)
    return mixture(normed, hsum, routes, gates, w_gate, w_up, w_down)


def solution(mesh):
    return jax.shard_map(
        shards,
        mesh=mesh,
        in_specs=(
            P("context", "tensor"),
            P("context", "tensor"),
            P("context", "tensor"),
            P(("context", "tensor"), None),
            P("tensor", "context"),
            P(),
            P(("context", "tensor"), None),
            P(("context", "tensor"), None),
            P("context", None, "tensor"),
            P("context", None, "tensor"),
            P("context", "tensor", None),
        ),
        out_specs=P(("context", "tensor"), None),
        check_vma=False,
    )
```

```python
import functools
import jax
import jax.numpy as jnp
from jax import lax
from jax.experimental import pallas as pl
from jax.experimental.pallas import tpu as pltpu
from jax.sharding import PartitionSpec as P

D = 4096
HW = 128
MESH = pl.DeviceIdType.MESH
BF = jnp.bfloat16
F32 = jnp.float32


def place():
    c = lax.axis_index("context")
    t = lax.axis_index("tensor")
    return c // 8, (c // 2) % 4, c % 2, t // 2, t % 2


def device(z, x, yl, yh, core):
    return {"context": z * 8 + x * 2 + yl, "tensor": yh * 2 + core}


def send(src, dst, ssem, rsem, to):
    copy = pltpu.make_async_remote_copy(
        src_ref=src, dst_ref=dst, send_sem=ssem, recv_sem=rsem, device_id=to, device_id_type=MESH
    )
    copy.start()
    return copy


def greet(peers):
    barrier = pltpu.get_barrier_semaphore()
    for peer in peers:
        pl.semaphore_signal(barrier, inc=1, device_id=peer, device_id_type=MESH)
    pl.semaphore_wait(barrier, len(peers))


def attention_kernel(
    q_ref, k_ref, v_ref, w_ref, resid_ref, gain_ref, hsum_ref, normed_ref,
    kall, vall, wall, att, scores, acc, sib_out, sib_in, own_out, own_in,
    k_s, k_r, v_s, v_r, w_s, w_r, a_s, a_r, c_s, c_r, o_s, o_r,
):
    z, x, yl, yh, core = place()
    ctx = z * 8 + x * 2 + yl
    zs = [lax.rem(z + o, 4) for o in range(4)]
    xs = [lax.rem(x + o, 4) for o in range(4)]
    group = [(o, p) for o in range(4) for p in range(2)][1:]
    sibling = device(z, x, yl, yh, 1 - core)
    z_peers = [device(zs[o], x, yl, yh, core) for o in (1, 2, 3)]
    x_peers = [device(z, xs[o], yl, yh, core) for o in (1, 2, 3)]
    y_peer = device(z, x, 1 - yl, yh, core)
    o_peers = [device(zs[o], x, yl, lax.rem(yh + p, 2), core) for o, p in group]
    greet([sibling, y_peer] + z_peers + x_peers + [device(zs[o], x, yl, 1 - yh, core) for o in range(4)])

    kall[z, x, yl] = k_ref[...]
    vall[z, x, yl] = v_ref[...]
    me = (z, x, yl)
    mine = pl.ds(pl.multiple_of((x * 2 + yl) * 128, 128), 128)
    both = pl.ds(pl.multiple_of(x * 256, 256), 256)
    low, high = pl.ds(0, 1024), pl.ds(1024, 1024)
    wall[:, mine] = w_ref[...]

    def wa1():
        return [send(w_ref.at[low], wall.at[low, mine], w_s.at[0], w_r.at[0], y_peer)]

    def wb1():
        return [
            send(w_ref.at[high], wall.at[high, mine], w_s.at[1 + i], w_r.at[1 + i], x_peers[i])
            for i in range(3)
        ]

    k1 = [send(kall.at[me], kall.at[me], k_s.at[i], k_r.at[i], z_peers[i]) for i in range(3)]
    v1 = [send(vall.at[me], vall.at[me], v_s.at[0], v_r.at[0], y_peer)]
    for copy in v1:
        copy.wait_recv()
    v2 = [
        send(vall.at[z, x], vall.at[z, x], v_s.at[1 + i], v_r.at[1 + i], x_peers[i])
        for i in range(3)
    ]
    v3 = []
    k3 = []

    def v_on(p, x_):
        for i in range(3):
            n = 4 + 3 * p + i
            v3.append(send(vall.at[z, x_], vall.at[z, x_], v_s.at[n], v_r.at[n], z_peers[i]))

    def k_on(p, x_):
        n = 6 + p
        k3.append(send(kall.at[:, x_, yl], kall.at[:, x_, yl], k_s.at[n], k_r.at[n], y_peer))

    v_on(0, x)
    for copy in k1:
        copy.wait_recv()
    k2 = [
        send(kall.at[:, x, yl], kall.at[:, x, yl], k_s.at[3 + i], k_r.at[3 + i], x_peers[i])
        for i in range(3)
    ]
    k_on(0, x)
    for i in range(3):
        x_ = lax.rem(x + 3 - i, 4)
        v2[i].wait_recv()
        v_on(1 + i, x_)
        k2[i].wait_recv()
        k_on(1 + i, x_)
    w1 = wb1() + wa1()
    w1[3].wait_recv()
    w2 = [
        send(wall.at[low, both], wall.at[low, both], w_s.at[4 + i], w_r.at[4 + i], x_peers[i])
        for i in range(3)
    ]

    def wb2(p, x_):
        cols = pl.ds(pl.multiple_of((x_ * 2 + yl) * 128, 128), 128)
        w2.append(send(wall.at[high, cols], wall.at[high, cols], w_s.at[7 + p], w_r.at[7 + p], y_peer))

    wb2(0, x)
    for copy in v3 + k3:
        copy.wait_recv()

    def forward():
        for i in range(3):
            w1[i].wait_recv()
            wb2(1 + i, lax.rem(x + 3 - i, 4))

    factor = HW**-0.5 * 1.4426950408889634
    last = ctx // 4
    nrow = 512

    def keys_of(ref, ch):
        return ref[ch // 2, pl.ds((ch % 2) * 2, 2)].reshape(512, HW)

    def columns(ch):
        return pl.ds(pl.multiple_of(ch * 512, 512), 512)

    def fold(f, s):
        return f(f(s[:, 0:128], s[:, 128:256]), f(s[:, 256:384], s[:, 384:512]))

    def heads(hc, carry):
        q = jnp.concatenate(
            [
                q_ref[:, pl.ds(pl.multiple_of(hc * 512 + i * HW, HW), HW)]
                for i in range(4)
            ],
            axis=0,
        )

        def product(ch):
            return lax.dot_general(
                q, keys_of(kall, ch), (((1,), (1,)), ((), ())), preferred_element_type=F32
            )

        def first(ch, top):
            s = product(ch)
            scores[:, columns(ch)] = s
            return jnp.maximum(top, fold(jnp.maximum, s))

        top = lax.fori_loop(0, last, first, jnp.full((nrow, 128), -jnp.inf, F32))
        s = product(last)
        row = lax.broadcasted_iota(jnp.int32, (nrow, 512), 0) % 128
        col = lax.broadcasted_iota(jnp.int32, (nrow, 512), 1)
        s = jnp.where(col <= row + (ctx % 4) * 128, s, -jnp.inf)
        scores[:, columns(last)] = s
        top = jnp.maximum(top, fold(jnp.maximum, s))
        shift = jnp.max(top, axis=1, keepdims=True) * factor

        def second(ch, carry):
            total, summed = carry
            p = jnp.exp2(scores[:, columns(ch)] * factor - shift)
            total = total + fold(jnp.add, p)
            summed = summed + jnp.dot(p.astype(BF), keys_of(vall, ch), preferred_element_type=F32)
            return total, summed

        zero = jnp.zeros((nrow, 128), F32)
        total, summed = lax.fori_loop(0, last + 1, second, (zero, zero))
        out = (summed / jnp.sum(total, axis=1, keepdims=True)).astype(BF)
        for i in range(4):
            att[z, hc, :, i * HW : (i + 1) * HW] = out[i * 128 : (i + 1) * 128]
        for i in range(3):
            send(att.at[z, hc], att.at[z, hc], a_s.at[hc, i], a_r.at[hc, i], z_peers[i])
        return carry

    lax.fori_loop(0, 1, heads, 0)
    forward()
    lax.fori_loop(1, 4, heads, 0)
    for copy in w2:
        copy.wait_recv()

    def project(hc, carry):
        for i in range(3):
            pltpu.make_async_remote_copy(
                src_ref=att.at[z, hc], dst_ref=att.at[z, hc], send_sem=a_s.at[hc, i],
                recv_sem=a_r.at[hc, i], device_id=z_peers[i], device_id_type=MESH,
            ).wait()
        a = att[:, hc].reshape(512, 512)
        for n in range(4):
            cols = slice(n * 256, (n + 1) * 256)
            r = jnp.dot(
                a, wall[pl.ds(pl.multiple_of(hc * 512, 512), 512), cols], preferred_element_type=F32
            ).reshape(4, 2, 2, 32, 256)
            acc[:, :, :, :, cols] = jnp.where(hc == 0, r, acc[:, :, :, :, cols] + r)
        return carry

    acc[...] = jnp.zeros_like(acc)
    lax.fori_loop(0, 4, project, 0)
    sib_out[...] = acc[:, :, 1 - core].astype(BF)
    copy = send(sib_out, sib_in, c_s.at[0], c_r.at[0], sibling)
    copy.wait()
    own_out[...] = (acc[:, :, core] + sib_in[...].astype(F32)).astype(BF)
    ocopies = []
    for i, (o, p) in enumerate(group):
        ocopies.append(
            send(
                own_out.at[zs[o], lax.rem(yh + p, 2)], own_in.at[z, yh], o_s.at[i], o_r.at[i], o_peers[i]
            )
        )
    own_in[z, yh] = own_out[z, yh]
    for copy in ocopies:
        copy.wait()
    square = jnp.zeros((32, 1), F32)
    for n in range(4):
        h = resid_ref[:, n * 1024 : (n + 1) * 1024].astype(F32) + (
            own_in[n, 0].astype(F32) + own_in[n, 1].astype(F32)
        )
        hsum_ref[n] = h
        square = square + jnp.sum(h * h, axis=1, keepdims=True)
    scale = lax.rsqrt(square * (1.0 / D) + 1e-06)
    for n in range(4):
        normed_ref[n] = (hsum_ref[n] * scale * gain_ref[:, n * 1024 : (n + 1) * 1024]).astype(BF)
    for copy in k1 + k2 + k3 + v1 + v2 + v3 + w1 + w2:
        copy.wait_send()


def attention(queries, keys, values, out_weight, resid, norm_gain):
    dma = pltpu.SemaphoreType.DMA
    vm = pl.BlockSpec(memory_space=pltpu.VMEM)
    return pl.pallas_call(
        attention_kernel,
        out_shape=(
            jax.ShapeDtypeStruct((4, 32, 1024), F32),
            jax.ShapeDtypeStruct((4, 32, 1024), BF),
        ),
        in_specs=[vm] * 6,
        out_specs=(vm, vm),
        scratch_shapes=[
            pltpu.VMEM((4, 4, 2, 128, 128), BF),
            pltpu.VMEM((4, 4, 2, 128, 128), BF),
            pltpu.VMEM((2048, 1024), BF),
            pltpu.VMEM((4, 4, 128, 512), BF),
            pltpu.VMEM((512, 4096), F32),
            pltpu.VMEM((4, 2, 2, 32, 1024), F32),
            pltpu.VMEM((4, 2, 32, 1024), BF),
            pltpu.VMEM((4, 2, 32, 1024), BF),
            pltpu.VMEM((4, 2, 32, 1024), BF),
            pltpu.VMEM((4, 2, 32, 1024), BF),
            dma((10,)), dma((10,)), dma((16,)), dma((16,)), dma((11,)), dma((11,)),
            dma((4, 3)), dma((4, 3)), dma((1,)), dma((1,)), dma((7,)), dma((7,)),
        ],
        compiler_params=pltpu.CompilerParams(
            collective_id=0, has_side_effects=True, vmem_limit_bytes=56 * 2**20
        ),
        cost_estimate=pl.CostEstimate(flops=8 * 10**9, bytes_accessed=4 * 2**20, transcendentals=8 * 2**20),
    )(queries, keys, values, out_weight, resid, norm_gain.reshape(1, D))


CH = 4
CW = D // CH
AHEAD = 2
BACK = 2


def experts_kernel(
    normed_ref, hsum_ref, routes_ref, gates_ref, wg_ref, wu_ref, wd_ref, out_ref,
    tok, meta, stage, rows, acc, hid, wgu, wdn, back, zin, uin, uhalf, vout, vin, pick, give,
    m_s, m_r, s1_s, s1_r, s2_s, s2_r, s3_s, s3_r, s4_s, s4_r,
    y_s, y_r, b3_s, b3_r, b2_s, b2_r, b1_s, b1_r, wg_m, wu_m, wd_m,
):
    z, x, yl, yh, core = place()
    y = yh * 2 + yl
    a = z * (1 - core) + x * core
    c = x * (1 - core) + z * core

    def at(a_, y_, c_):
        return device(
            a_ * (1 - core) + c_ * core, c_ * (1 - core) + a_ * core, y_ % 2, y_ // 2, core
        )

    As = [lax.rem(a + o, 4) for o in range(4)]
    Ys = [lax.rem(y + o, 4) for o in range(4)]
    Cs = [lax.rem(c + o, 4) for o in range(4)]
    a_peers = [at(As[o], y, c) for o in (1, 2, 3)]
    y_peers = [at(a, Ys[o], c) for o in (1, 2, 3)]
    c_peers = [at(a, y, Cs[o]) for o in (1, 2, 3)]
    sibling = device(z, x, yl, yh, 1 - core)
    greet([sibling] + a_peers + y_peers + c_peers)

    def remote(src, dst, ssem, rsem, to):
        return pltpu.make_async_remote_copy(
            src_ref=src, dst_ref=dst, send_sem=ssem, recv_sem=rsem, device_id=to, device_id_type=MESH
        )

    def m1(i):
        return remote(meta.at[y, a], meta.at[y, a], m_s.at[i], m_r.at[i], a_peers[i])

    def m2(i):
        return remote(meta.at[y], meta.at[y], m_s.at[3 + i], m_r.at[3 + i], y_peers[i])

    def s1(q, i):
        return remote(normed_ref.at[q], tok.at[q, y, a], s1_s.at[q, i], s1_r.at[q, i], a_peers[i])

    ends = (y_peers[0], y_peers[2])
    Yn = (Ys[1], Ys[3])
    parts = (pl.ds(0, 2), pl.ds(2, 2))

    def s2(q, i):
        return remote(tok.at[q, y], tok.at[q, y], s2_s.at[q, i], s2_r.at[q, i], ends[i])

    def relay(q, i):
        block = tok.at[q, Yn[1 - i], parts[i]]
        return remote(block, block, s2_s.at[q, 2 + i], s2_r.at[q, 2 + i], ends[i])

    def s3(q, i):
        return remote(
            stage.at[q, i], rows.at[q, 0, :, c], s3_s.at[q, i], s3_r.at[q, i], c_peers[i]
        )

    def s4(q):
        return remote(rows.at[q, 0], rows.at[q, 1], s4_s.at[q], s4_r.at[q], sibling)

    def yb(q):
        return remote(rows.at[q, 1], back.at[q], y_s.at[q], y_r.at[q], sibling)

    def b3(q, i):
        return remote(
            rows.at[q, 0, :, Cs[i + 1]], zin.at[q, c], b3_s.at[q, i], b3_r.at[q, i], c_peers[i]
        )

    def b2(q, i):
        return remote(tok.at[q, Yn[i]], uin.at[q, i], b2_s.at[q, i], b2_r.at[q, i], ends[i])

    def far(q, i):
        block = tok.at[q, Ys[2], parts[i]]
        return remote(block, uhalf.at[q, i], b2_s.at[q, 2 + i], b2_r.at[q, 2 + i], ends[i])

    def b1(q, i):
        return remote(vout.at[q, As[i + 1]], vin.at[q, a], b1_s.at[q, i], b1_r.at[q, i], a_peers[i])

    def load_up(q):
        slot = q % 2
        depth = pl.ds(pl.multiple_of(q * CW, CW), CW)
        return (
            pltpu.make_async_copy(wg_ref.at[:, depth], wgu.at[slot, :, :, 0:384], wg_m.at[slot]),
            pltpu.make_async_copy(wu_ref.at[:, depth], wgu.at[slot, :, :, 384:768], wu_m.at[slot]),
        )

    def load_down(q):
        cols = pl.ds(pl.multiple_of(q * CW, CW), CW)
        return pltpu.make_async_copy(wd_ref.at[:, :, cols], wdn.at[q % 3], wd_m.at[q % 3])

    lane = lax.broadcasted_iota(jnp.int32, (32, 128), 1)
    named = jnp.zeros((32, 128), F32)
    gate = jnp.zeros((32, 128), F32)
    for k in range(8):
        hit = routes_ref[:, k : k + 1] == lane % 64
        named = named + jnp.where(hit, 1.0, 0.0)
        gate = gate + jnp.where(hit, gates_ref[:, k : k + 1], 0.0)
    before = (
        lax.broadcasted_iota(jnp.int32, (32, 32), 1) < lax.broadcasted_iota(jnp.int32, (32, 32), 0)
    )
    rank = jnp.dot(
        jnp.where(before, 1.0, 0.0).astype(BF), named.astype(BF), preferred_element_type=F32
    )
    meta[y, a] = jnp.where(lane < 64, jnp.where(named > 0.5, rank, -1.0), gate).astype(BF)
    for i in range(3):
        m1(i).start()

    def first(q, carry):
        tok[q, y, a] = normed_ref[q]
        for i in range(3):
            s1(q, i).start()
        return carry

    lax.fori_loop(0, CH, first, 0)
    for q in range(2):
        for copy in load_up(q):
            copy.start()
    for q in range(3):
        load_down(q).start()
    for i in range(3):
        m1(i).wait()
    for i in range(3):
        m2(i).start()

    def second(q):
        for i in range(3):
            s1(q, i).wait()
        for i in range(2):
            s2(q, i).start()

    for q in range(AHEAD):
        second(q)
    for i in range(3):
        m2(i).wait()

    info = meta[...].reshape(512, 128)
    base = a * (16 * (1 - core) + 4 * core) + 2 * yl
    step_c = 4 * (1 - core) + 16 * core
    m_lane = lax.broadcasted_iota(jnp.int32, (128, 128), 1)
    l_row = lax.broadcasted_iota(jnp.int32, (128, 128), 0)
    want = base + (m_lane // 2) * step_c + m_lane % 2
    pick_rank = jnp.where((l_row == want) & (m_lane < 8), 1.0, 0.0).astype(BF)
    pick_gate = jnp.where((l_row == want + 64) & (m_lane < 8), 1.0, 0.0).astype(BF)
    rank_col = jnp.dot(info, pick_rank, preferred_element_type=F32)
    gate_col = jnp.dot(info, pick_gate, preferred_element_type=F32)
    m_row = lax.broadcasted_iota(jnp.int32, (16, 128), 0)
    l_lane = lax.broadcasted_iota(jnp.int32, (16, 128), 1)
    pick_row = jnp.where(
        l_lane == base + (m_row // 2) * step_c + m_row % 2, 1.0, 0.0
    ).astype(BF)
    rank_row = lax.dot_general(
        pick_row, info, (((1,), (1,)), ((), ())), preferred_element_type=F32
    )
    src_row = (lax.broadcasted_iota(jnp.int32, (16, 512), 1) // 32).astype(F32)
    code_row = jnp.where(rank_row > -0.5, src_row * 6.0 + rank_row, -1.0)
    src_col = (lax.broadcasted_iota(jnp.int32, (512, 128), 0) // 32).astype(F32)
    code_col = jnp.where(rank_col > -0.5, src_col * 6.0 + rank_col, -1000.0)
    at_row = lax.broadcasted_iota(jnp.int32, (96, 512), 0).astype(F32)
    at_col = lax.broadcasted_iota(jnp.int32, (512, 768), 1).astype(F32)
    weight = jnp.zeros((512, 768), F32)
    for m in range(8):
        pick[m // 2, (m % 2) * 96 : (m % 2 + 1) * 96] = jnp.where(
            at_row == code_row[m : m + 1], 1.0, 0.0
        ).astype(BF)
        weight = weight + jnp.where(
            at_col == code_col[:, m : m + 1] + (96.0 * m), gate_col[:, m : m + 1], 0.0
        )
    give[...] = weight.astype(BF)

    def pass_on(q):
        for i in range(2):
            s2(q, i).wait_recv()
        for i in range(2):
            relay(q, i).start()

        @pl.when(q + AHEAD < CH)
        def _():
            second(q + AHEAD)

    def select(q):
        for i in range(2):
            relay(q, i).wait_recv()

        def one(o):
            p = pick[lax.rem(c + o, 4)]
            parts = [
                jnp.dot(
                    p,
                    tok[q, :, :, :, n * 256 : (n + 1) * 256].reshape(512, 256),
                    preferred_element_type=F32,
                ).astype(BF).reshape(2, 96, 256)
                for n in range(CW // 256)
            ]
            return parts

        def other(i, carry):
            for n, part in enumerate(one(i + 1)):
                stage[q, i, :, :, n * 256 : (n + 1) * 256] = part
            return carry

        lax.fori_loop(0, 3, other, 0)
        for i in range(3):
            s3(q, i).start()
        for n, part in enumerate(one(0)):
            rows[q, 0, :, c, :, n * 256 : (n + 1) * 256] = part

    def share(q):
        for i in range(3):
            s3(q, i).wait_recv()
        s4(q).start()

    def up(q):
        for copy in load_up(q):
            copy.wait()
        s4(q).wait_recv()
        slot = q % 2

        def one(i, carry):
            s, j = i // 2, i % 2
            r = rows[q, s, j].reshape(384, CW)
            for n in range(3):
                cols = slice(n * 256, (n + 1) * 256)
                d = jnp.dot(r, wgu[slot, j, :, cols], preferred_element_type=F32)
                acc[s, j, :, cols] = acc[s, j, :, cols] + d
            return carry

        lax.fori_loop(0, 4, one, 0)

        @pl.when(q < CH - 2)
        def _():
            for copy in load_up(q + 2):
                copy.start()

    acc[...] = jnp.zeros_like(acc)

    def dispatch(step, carry):
        @pl.when(step < CH)
        def _():
            pass_on(step)

        @pl.when((step >= 1) & (step < CH + 1))
        def _():
            select(step - 1)

        @pl.when((step >= 2) & (step < CH + 2))
        def _():
            share(step - 2)

        @pl.when(step >= 3)
        def _():
            up(step - 3)

        return carry

    lax.fori_loop(0, CH + 3, dispatch, 0)

    def activate(i, carry):
        s, j = i // 2, i % 2
        v = acc[s, j, :, 0:384]
        hid[s, j] = (v / (1.0 + jnp.exp(-v)) * acc[s, j, :, 384:768]).astype(BF)
        return carry

    lax.fori_loop(0, 4, activate, 0)

    def down(q, s, j, n):
        return jnp.dot(
            hid[s, j], wdn[lax.rem(q, 3), j, :, n * 256 : (n + 1) * 256], preferred_element_type=F32
        )

    def half(step, carry):
        @pl.when(step < CH)
        def _():
            load_down(step).wait()

            def one(j, carry):
                for n in range(CW // 256):
                    rows[step, 1, j, :, :, n * 256 : (n + 1) * 256] = (
                        down(step, 1, j, n).astype(BF).reshape(4, 96, 256)
                    )
                return carry

            lax.fori_loop(0, 2, one, 0)
            yb(step).start()

        @pl.when(step >= 1)
        def _():
            q = step - 1
            s4(q).wait_send()
            yb(q).wait_recv()

            def one(j, carry):
                for n in range(CW // 256):
                    cols = slice(n * 256, (n + 1) * 256)
                    v = down(q, 0, j, n).reshape(4, 96, 256) + back[q, j, :, :, cols].astype(F32)
                    rows[q, 0, j, :, :, cols] = v.astype(BF)
                return carry

            lax.fori_loop(0, 2, one, 0)
            @pl.when(q < BACK)
            def _():
                for i in range(3):
                    b3(q, i).start()

            zin[q, c] = rows[q, 0, :, c]

            @pl.when(q < CH - 3)
            def _():
                load_down(q + 3).start()

        return carry

    lax.fori_loop(0, CH + 1, half, 0)

    def one_sum(q, o):
        y_ = Ys[o]
        g = give[pl.ds(pl.multiple_of(y_ * 128, 128), 128)]
        for n in range(CW // 256):
            cols = slice(n * 256, (n + 1) * 256)
            tok[q, y_, :, :, cols] = jnp.dot(
                g, zin[q, :, :, :, cols].reshape(768, 256), preferred_element_type=F32
            ).astype(BF).reshape(4, 32, 256)

    def gather_sums(q):
        for i in range(3):
            b3(q, i).wait_recv()

        @pl.when(q + BACK < CH)
        def _():
            for i in range(3):
                b3(q + BACK, i).start()

        for i in range(2):
            s2(q, i).wait_send()
            relay(q, i).wait_send()
        one_sum(q, 2)
        for i in range(2):
            far(q, i).start()
        for o in (1, 3, 0):
            one_sum(q, o)

    def add_half(q):
        for i in range(2):
            far(q, i).wait_recv()
            block = tok[q, Yn[i], parts[i]].astype(F32) + uhalf[q, i].astype(F32)
            tok[q, Yn[i], parts[i]] = block.astype(BF)
            b2(q, i).start()

    def along(q):
        for i in range(2):
            b2(q, i).wait_recv()
        v = uin[q, 0].astype(F32) + uin[q, 1].astype(F32) + tok[q, y].astype(F32)
        vout[q] = v.astype(BF)
        for i in range(3):
            b1(q, i).start()
        vin[q, a] = vout[q, a]

    def store(q):
        for i in range(3):
            b1(q, i).wait_recv()
        v = vin[q, 0].astype(F32) + vin[q, 1].astype(F32)
        v = v + vin[q, 2].astype(F32) + vin[q, 3].astype(F32)
        out_ref[:, pl.ds(pl.multiple_of(q * CW, CW), CW)] = (hsum_ref[q] + v).astype(BF)

    def combine(step, carry):
        @pl.when((step >= 1) & (step < CH + 1))
        def _():
            add_half(step - 1)

        @pl.when(step < CH)
        def _():
            gather_sums(step)

        @pl.when((step >= 2) & (step < CH + 2))
        def _():
            along(step - 2)

        @pl.when(step >= 3)
        def _():
            store(step - 3)

        return carry

    lax.fori_loop(0, CH + 3, combine, 0)

    def finish(q, carry):
        yb(q).wait_send()
        for i in range(3):
            s3(q, i).wait_send()
            b3(q, i).wait_send()
            b1(q, i).wait_send()
        for i in range(2):
            far(q, i).wait_send()
            b2(q, i).wait_send()
        return carry

    lax.fori_loop(0, CH, finish, 0)


def mixture(normed, hsum, routes, gates, w_gate, w_up, w_down):
    dma = pltpu.SemaphoreType.DMA
    vm = pl.BlockSpec(memory_space=pltpu.VMEM)
    hbm = pl.BlockSpec(memory_space=pl.ANY)
    return pl.pallas_call(
        experts_kernel,
        out_shape=jax.ShapeDtypeStruct((32, D), BF),
        in_specs=[vm] * 4 + [hbm] * 3,
        out_specs=vm,
        scratch_shapes=[
            pltpu.VMEM((CH, 4, 4, 32, CW), BF),
            pltpu.VMEM((4, 4, 32, 128), BF),
            pltpu.VMEM((CH, 3, 2, 96, CW), BF),
            pltpu.VMEM((CH, 2, 2, 4, 96, CW), BF),
            pltpu.VMEM((2, 2, 384, 768), F32),
            pltpu.VMEM((2, 2, 384, 384), BF),
            pltpu.VMEM((2, 2, CW, 768), BF),
            pltpu.VMEM((3, 2, 384, CW), BF),
            pltpu.VMEM((CH, 2, 4, 96, CW), BF),
            pltpu.VMEM((CH, 4, 2, 96, CW), BF),
            pltpu.VMEM((CH, 2, 4, 32, CW), BF),
            pltpu.VMEM((CH, 2, 2, 32, CW), BF),
            pltpu.VMEM((CH, 4, 32, CW), BF),
            pltpu.VMEM((CH, 4, 32, CW), BF),
            pltpu.VMEM((4, 192, 512), BF),
            pltpu.VMEM((512, 768), BF),
            dma((6,)), dma((6,)),
            dma((CH, 3)), dma((CH, 3)), dma((CH, 4)), dma((CH, 4)), dma((CH, 3)), dma((CH, 3)),
            dma((CH,)), dma((CH,)), dma((CH,)), dma((CH,)),
            dma((CH, 3)), dma((CH, 3)), dma((CH, 4)), dma((CH, 4)), dma((CH, 3)), dma((CH, 3)),
            dma((2,)), dma((2,)), dma((3,)),
        ],
        compiler_params=pltpu.CompilerParams(
            collective_id=1, has_side_effects=True, vmem_limit_bytes=63 * 2**20
        ),
        cost_estimate=pl.CostEstimate(
            flops=20 * 10**9, bytes_accessed=20 * 2**20, transcendentals=2**20
        ),
    )(normed, hsum, routes, gates, w_gate, w_up, w_down)


def shards(
    queries, keys, values, resid, out_weight, norm_gain, routes, gates, w_gate, w_up, w_down
):
    hsum, normed = attention(queries, keys, values, out_weight, resid, norm_gain)
    return mixture(normed, hsum, routes, gates, w_gate, w_up, w_down)


def solution(mesh):
    return jax.shard_map(
        shards,
        mesh=mesh,
        in_specs=(
            P("context", "tensor"),
            P("context", "tensor"),
            P("context", "tensor"),
            P(("context", "tensor"), None),
            P("tensor", "context"),
            P(),
            P(("context", "tensor"), None),
            P(("context", "tensor"), None),
            P("context", None, "tensor"),
            P("context", None, "tensor"),
            P("context", "tensor", None),
        ),
        out_specs=P(("context", "tensor"), None),
        check_vma=False,
    )
```

```python
import functools
import jax
import jax.numpy as jnp
from jax import lax
from jax.experimental import pallas as pl
from jax.experimental.pallas import tpu as pltpu
from jax.sharding import PartitionSpec as P

D = 4096
HW = 128
MESH = pl.DeviceIdType.MESH
BF = jnp.bfloat16
F32 = jnp.float32


def place():
    c = lax.axis_index("context")
    t = lax.axis_index("tensor")
    return c // 8, (c // 2) % 4, c % 2, t // 2, t % 2


def device(z, x, yl, yh, core):
    return {"context": z * 8 + x * 2 + yl, "tensor": yh * 2 + core}


def send(src, dst, ssem, rsem, to):
    copy = pltpu.make_async_remote_copy(
        src_ref=src, dst_ref=dst, send_sem=ssem, recv_sem=rsem, device_id=to, device_id_type=MESH
    )
    copy.start()
    return copy


def greet(peers):
    barrier = pltpu.get_barrier_semaphore()
    for peer in peers:
        pl.semaphore_signal(barrier, inc=1, device_id=peer, device_id_type=MESH)
    pl.semaphore_wait(barrier, len(peers))


def attention_kernel(
    q_ref, k_ref, v_ref, w_ref, resid_ref, gain_ref, hsum_ref, normed_ref,
    kall, vall, wall, att, scores, acc, sib_out, sib_in, own_out, own_in,
    k_s, k_r, v_s, v_r, w_s, w_r, a_s, a_r, c_s, c_r, o_s, o_r,
):
    z, x, yl, yh, core = place()
    ctx = z * 8 + x * 2 + yl
    zs = [lax.rem(z + o, 4) for o in range(4)]
    xs = [lax.rem(x + o, 4) for o in range(4)]
    group = [(o, p) for o in range(4) for p in range(2)][1:]
    sibling = device(z, x, yl, yh, 1 - core)
    z_peers = [device(zs[o], x, yl, yh, core) for o in (1, 2, 3)]
    x_peers = [device(z, xs[o], yl, yh, core) for o in (1, 2, 3)]
    y_peer = device(z, x, 1 - yl, yh, core)
    o_peers = [device(zs[o], x, yl, lax.rem(yh + p, 2), core) for o, p in group]
    greet([sibling, y_peer] + z_peers + x_peers + [device(zs[o], x, yl, 1 - yh, core) for o in range(4)])

    kall[z, x, yl] = k_ref[...]
    vall[z, x, yl] = v_ref[...]
    me = (z, x, yl)
    mine = pl.ds(pl.multiple_of((x * 2 + yl) * 128, 128), 128)
    both = pl.ds(pl.multiple_of(x * 256, 256), 256)
    low, high = pl.ds(0, 1024), pl.ds(1024, 1024)
    wall[:, mine] = w_ref[...]

    def wa1():
        return [send(w_ref.at[low], wall.at[low, mine], w_s.at[0], w_r.at[0], y_peer)]

    def wb1():
        return [
            send(w_ref.at[high], wall.at[high, mine], w_s.at[1 + i], w_r.at[1 + i], x_peers[i])
            for i in range(3)
        ]

    k1 = [send(kall.at[me], kall.at[me], k_s.at[i], k_r.at[i], z_peers[i]) for i in range(3)]
    v1 = [send(vall.at[me], vall.at[me], v_s.at[0], v_r.at[0], y_peer)]
    for copy in v1:
        copy.wait_recv()
    v2 = [
        send(vall.at[z, x], vall.at[z, x], v_s.at[1 + i], v_r.at[1 + i], x_peers[i])
        for i in range(3)
    ]
    v3 = []
    k3 = []

    def v_on(p, x_):
        for i in range(3):
            n = 4 + 3 * p + i
            v3.append(send(vall.at[z, x_], vall.at[z, x_], v_s.at[n], v_r.at[n], z_peers[i]))

    def k_on(p, x_):
        n = 6 + p
        k3.append(send(kall.at[:, x_, yl], kall.at[:, x_, yl], k_s.at[n], k_r.at[n], y_peer))

    v_on(0, x)
    for copy in k1:
        copy.wait_recv()
    k2 = [
        send(kall.at[:, x, yl], kall.at[:, x, yl], k_s.at[3 + i], k_r.at[3 + i], x_peers[i])
        for i in range(3)
    ]
    k_on(0, x)
    for i in range(3):
        x_ = lax.rem(x + 3 - i, 4)
        v2[i].wait_recv()
        v_on(1 + i, x_)
        k2[i].wait_recv()
        k_on(1 + i, x_)
    w1 = wb1() + wa1()
    w1[3].wait_recv()
    w2 = [
        send(wall.at[low, both], wall.at[low, both], w_s.at[4 + i], w_r.at[4 + i], x_peers[i])
        for i in range(3)
    ]

    def wb2(p, x_):
        cols = pl.ds(pl.multiple_of((x_ * 2 + yl) * 128, 128), 128)
        w2.append(send(wall.at[high, cols], wall.at[high, cols], w_s.at[7 + p], w_r.at[7 + p], y_peer))

    wb2(0, x)
    for copy in v3 + k3:
        copy.wait_recv()

    def forward():
        for i in range(3):
            w1[i].wait_recv()
            wb2(1 + i, lax.rem(x + 3 - i, 4))

    factor = HW**-0.5 * 1.4426950408889634
    last = ctx // 4
    nrow = 512

    def keys_of(ref, ch):
        return ref[ch // 2, pl.ds((ch % 2) * 2, 2)].reshape(512, HW)

    def columns(ch):
        return pl.ds(pl.multiple_of(ch * 512, 512), 512)

    def fold(f, s):
        return f(f(s[:, 0:128], s[:, 128:256]), f(s[:, 256:384], s[:, 384:512]))

    def heads(hc, carry):
        q = jnp.concatenate(
            [
                q_ref[:, pl.ds(pl.multiple_of(hc * 512 + i * HW, HW), HW)]
                for i in range(4)
            ],
            axis=0,
        )

        def product(ch):
            return lax.dot_general(
                q, keys_of(kall, ch), (((1,), (1,)), ((), ())), preferred_element_type=F32
            )

        def first(ch, top):
            s = product(ch)
            scores[:, columns(ch)] = s
            return jnp.maximum(top, fold(jnp.maximum, s))

        top = lax.fori_loop(0, last, first, jnp.full((nrow, 128), -jnp.inf, F32))
        s = product(last)
        row = lax.broadcasted_iota(jnp.int32, (nrow, 512), 0) % 128
        col = lax.broadcasted_iota(jnp.int32, (nrow, 512), 1)
        s = jnp.where(col <= row + (ctx % 4) * 128, s, -jnp.inf)
        scores[:, columns(last)] = s
        top = jnp.maximum(top, fold(jnp.maximum, s))
        shift = jnp.max(top, axis=1, keepdims=True) * factor

        def second(ch, carry):
            total, summed = carry
            p = jnp.exp2(scores[:, columns(ch)] * factor - shift)
            total = total + fold(jnp.add, p)
            summed = summed + jnp.dot(p.astype(BF), keys_of(vall, ch), preferred_element_type=F32)
            return total, summed

        zero = jnp.zeros((nrow, 128), F32)
        total, summed = lax.fori_loop(0, last + 1, second, (zero, zero))
        out = (summed / jnp.sum(total, axis=1, keepdims=True)).astype(BF)
        for i in range(4):
            att[z, hc, :, i * HW : (i + 1) * HW] = out[i * 128 : (i + 1) * 128]
        for i in range(3):
            send(att.at[z, hc], att.at[z, hc], a_s.at[hc, i], a_r.at[hc, i], z_peers[i])
        return carry

    lax.fori_loop(0, 1, heads, 0)
    forward()
    lax.fori_loop(1, 4, heads, 0)
    for copy in w2:
        copy.wait_recv()

    def project(hc, carry):
        for i in range(3):
            pltpu.make_async_remote_copy(
                src_ref=att.at[z, hc], dst_ref=att.at[z, hc], send_sem=a_s.at[hc, i],
                recv_sem=a_r.at[hc, i], device_id=z_peers[i], device_id_type=MESH,
            ).wait()
        a = att[:, hc].reshape(512, 512)
        for n in range(4):
            cols = slice(n * 256, (n + 1) * 256)
            r = jnp.dot(
                a, wall[pl.ds(pl.multiple_of(hc * 512, 512), 512), cols], preferred_element_type=F32
            ).reshape(4, 2, 2, 32, 256)
            acc[:, :, :, :, cols] = jnp.where(hc == 0, r, acc[:, :, :, :, cols] + r)
        return carry

    acc[...] = jnp.zeros_like(acc)
    lax.fori_loop(0, 4, project, 0)
    sib_out[...] = acc[:, :, 1 - core].astype(BF)
    copy = send(sib_out, sib_in, c_s.at[0], c_r.at[0], sibling)
    copy.wait()
    own_out[...] = (acc[:, :, core] + sib_in[...].astype(F32)).astype(BF)
    ocopies = []
    for i, (o, p) in enumerate(group):
        ocopies.append(
            send(
                own_out.at[zs[o], lax.rem(yh + p, 2)], own_in.at[z, yh], o_s.at[i], o_r.at[i], o_peers[i]
            )
        )
    own_in[z, yh] = own_out[z, yh]
    for copy in ocopies:
        copy.wait()
    square = jnp.zeros((32, 1), F32)
    for n in range(8):
        at, cols = n // 2, slice((n % 2) * 512, (n % 2 + 1) * 512)
        h = resid_ref[:, n * 512 : (n + 1) * 512].astype(F32) + (
            own_in[at, 0, :, cols].astype(F32) + own_in[at, 1, :, cols].astype(F32)
        )
        hsum_ref[n] = h
        square = square + jnp.sum(h * h, axis=1, keepdims=True)
    scale = lax.rsqrt(square * (1.0 / D) + 1e-06)
    for n in range(8):
        normed_ref[n] = (hsum_ref[n] * scale * gain_ref[:, n * 512 : (n + 1) * 512]).astype(BF)
    for copy in k1 + k2 + k3 + v1 + v2 + v3 + w1 + w2:
        copy.wait_send()


def attention(queries, keys, values, out_weight, resid, norm_gain):
    dma = pltpu.SemaphoreType.DMA
    vm = pl.BlockSpec(memory_space=pltpu.VMEM)
    return pl.pallas_call(
        attention_kernel,
        out_shape=(
            jax.ShapeDtypeStruct((8, 32, 512), F32),
            jax.ShapeDtypeStruct((8, 32, 512), BF),
        ),
        in_specs=[vm] * 6,
        out_specs=(vm, vm),
        scratch_shapes=[
            pltpu.VMEM((4, 4, 2, 128, 128), BF),
            pltpu.VMEM((4, 4, 2, 128, 128), BF),
            pltpu.VMEM((2048, 1024), BF),
            pltpu.VMEM((4, 4, 128, 512), BF),
            pltpu.VMEM((512, 4096), F32),
            pltpu.VMEM((4, 2, 2, 32, 1024), F32),
            pltpu.VMEM((4, 2, 32, 1024), BF),
            pltpu.VMEM((4, 2, 32, 1024), BF),
            pltpu.VMEM((4, 2, 32, 1024), BF),
            pltpu.VMEM((4, 2, 32, 1024), BF),
            dma((10,)), dma((10,)), dma((16,)), dma((16,)), dma((11,)), dma((11,)),
            dma((4, 3)), dma((4, 3)), dma((1,)), dma((1,)), dma((7,)), dma((7,)),
        ],
        compiler_params=pltpu.CompilerParams(
            collective_id=0, has_side_effects=True, vmem_limit_bytes=56 * 2**20
        ),
        cost_estimate=pl.CostEstimate(flops=8 * 10**9, bytes_accessed=4 * 2**20, transcendentals=8 * 2**20),
    )(queries, keys, values, out_weight, resid, norm_gain.reshape(1, D))


CH = 8
CW = D // CH
OUT = tuple((q, 1) for q in range(8))
HOME = ((0, 2), (2, 2), (4, 2), (6, 2))
NO, NH = len(OUT), len(HOME)
AHEAD = 2
BACK = 2


def experts_kernel(
    normed_ref, hsum_ref, routes_ref, gates_ref, wg_ref, wu_ref, wd_ref, out_ref,
    tok, meta, stage, rows, acc, hid, wgu, wdn, back, zin, uin, uhalf, vout, vin, pick, give,
    m_s, m_r, s1_s, s1_r, s2_s, s2_r, s3_s, s3_r, s4_s, s4_r,
    y_s, y_r, b3_s, b3_r, b2_s, b2_r, b1_s, b1_r, wg_m, wu_m, wd_m,
):
    z, x, yl, yh, core = place()
    y = yh * 2 + yl
    a = z * (1 - core) + x * core
    c = x * (1 - core) + z * core

    def at(a_, y_, c_):
        return device(
            a_ * (1 - core) + c_ * core, c_ * (1 - core) + a_ * core, y_ % 2, y_ // 2, core
        )

    As = [lax.rem(a + o, 4) for o in range(4)]
    Ys = [lax.rem(y + o, 4) for o in range(4)]
    Cs = [lax.rem(c + o, 4) for o in range(4)]
    a_peers = [at(As[o], y, c) for o in (1, 2, 3)]
    y_peers = [at(a, Ys[o], c) for o in (1, 2, 3)]
    c_peers = [at(a, y, Cs[o]) for o in (1, 2, 3)]
    sibling = device(z, x, yl, yh, 1 - core)
    greet([sibling] + a_peers + y_peers + c_peers)

    def un(g, groups=OUT):
        return pl.ds(*groups[g])

    def remote(src, dst, ssem, rsem, to):
        return pltpu.make_async_remote_copy(
            src_ref=src, dst_ref=dst, send_sem=ssem, recv_sem=rsem, device_id=to, device_id_type=MESH
        )

    def m1(i):
        return remote(meta.at[y, a], meta.at[y, a], m_s.at[i], m_r.at[i], a_peers[i])

    def m2(i):
        return remote(meta.at[y], meta.at[y], m_s.at[3 + i], m_r.at[3 + i], y_peers[i])

    def s1(g, i):
        u = un(g)
        return remote(normed_ref.at[u], tok.at[u, y, a], s1_s.at[g, i], s1_r.at[g, i], a_peers[i])

    ends = (y_peers[0], y_peers[2])
    Yn = (Ys[1], Ys[3])
    parts = (pl.ds(0, 2), pl.ds(2, 2))

    def s2(g, i):
        block = tok.at[un(g), y]
        return remote(block, block, s2_s.at[g, i], s2_r.at[g, i], ends[i])

    def relay(g, i):
        block = tok.at[un(g), Yn[1 - i], parts[i]]
        return remote(block, block, s2_s.at[g, 2 + i], s2_r.at[g, 2 + i], ends[i])

    def s3(g, i):
        u = un(g)
        return remote(
            stage.at[u, i], rows.at[u, 0, :, c], s3_s.at[g, i], s3_r.at[g, i], c_peers[i]
        )

    def s4(g):
        u = un(g)
        return remote(rows.at[u, 0], rows.at[u, 1], s4_s.at[g], s4_r.at[g], sibling)

    def yb(g):
        u = un(g, HOME)
        return remote(rows.at[u, 1], back.at[u], y_s.at[g], y_r.at[g], sibling)

    def b3(g, i):
        u = un(g, HOME)
        return remote(
            rows.at[u, 0, :, Cs[i + 1]], zin.at[u, c], b3_s.at[g, i], b3_r.at[g, i], c_peers[i]
        )

    def b2(g, i):
        u = un(g, HOME)
        return remote(tok.at[u, Yn[i]], uin.at[u, i], b2_s.at[g, i], b2_r.at[g, i], ends[i])

    def far(g, i):
        u = un(g, HOME)
        block = tok.at[u, Ys[2], parts[i]]
        return remote(block, uhalf.at[u, i], b2_s.at[g, 2 + i], b2_r.at[g, 2 + i], ends[i])

    def b1(g, i):
        u = un(g, HOME)
        return remote(vout.at[u, As[i + 1]], vin.at[u, a], b1_s.at[g, i], b1_r.at[g, i], a_peers[i])

    def units(g, body, groups=HOME):
        q, n = groups[g]

        def one(u, carry):
            body(u)
            return carry

        if n == 1:
            body(q)
        else:
            lax.fori_loop(q, q + n, one, 0)

    def load_up(g):
        q, n = OUT[g]
        slot, depth, held = g % 2, pl.ds(q * CW, n * CW), pl.ds(0, n * CW)
        return (
            pltpu.make_async_copy(wg_ref.at[:, depth], wgu.at[slot, :, held, 0:384], wg_m.at[slot]),
            pltpu.make_async_copy(
                wu_ref.at[:, depth], wgu.at[slot, :, held, 384:768], wu_m.at[slot]
            ),
        )

    def load_down(q):
        return pltpu.make_async_copy(
            wd_ref.at[:, :, q * CW : (q + 1) * CW], wdn.at[q], wd_m.at[q]
        )

    lane = lax.broadcasted_iota(jnp.int32, (32, 128), 1)
    expert = (lane % 64).astype(F32)
    same = lax.broadcasted_iota(jnp.int32, (32, 32), 0) == lax.broadcasted_iota(
        jnp.int32, (32, 32), 1
    )
    turn = jnp.where(same, 1.0, 0.0).astype(BF)
    across = (((1,), (1,)), ((), ()))
    route_col = lax.dot_general(
        turn, routes_ref[...].astype(F32).astype(BF), across, preferred_element_type=F32
    )
    gate_own = lax.dot_general(
        turn, gates_ref[...].astype(BF), across, preferred_element_type=F32
    )
    named = jnp.zeros((32, 128), F32)
    gate = jnp.zeros((32, 128), F32)
    for k in range(8):
        hit = route_col[:, k : k + 1] == expert
        named = named + jnp.where(hit, 1.0, 0.0)
        gate = gate + jnp.where(hit, gate_own[:, k : k + 1], 0.0)
    before = (
        lax.broadcasted_iota(jnp.int32, (32, 32), 1) < lax.broadcasted_iota(jnp.int32, (32, 32), 0)
    )
    rank = jnp.dot(
        jnp.where(before, 1.0, 0.0).astype(BF), named.astype(BF), preferred_element_type=F32
    )
    meta[y, a] = jnp.where(lane < 64, jnp.where(named > 0.5, rank, -1.0), gate).astype(BF)
    tok[:, y, a] = normed_ref[...]
    for i in range(3):
        s1(0, i).start()
    for i in range(3):
        m1(i).start()
    for g in range(2):
        for copy in load_up(g):
            copy.start()
    for q in range(CH):
        load_down(q).start()

    def second(g):
        for i in range(3):
            s1(g, i).wait()
        for i in range(2):
            s2(g, i).start()

    second(0)
    for g in range(1, NO):
        for i in range(3):
            s1(g, i).start()
    for i in range(3):
        m1(i).wait()
    for i in range(3):
        m2(i).start()
    for g in range(1, AHEAD):
        second(g)
    for i in range(3):
        m2(i).wait()

    info = meta[...].reshape(512, 128)
    base = a * (16 * (1 - core) + 4 * core) + 2 * yl
    step_c = 4 * (1 - core) + 16 * core
    m_lane = lax.broadcasted_iota(jnp.int32, (128, 128), 1)
    l_row = lax.broadcasted_iota(jnp.int32, (128, 128), 0)
    want = base + (m_lane // 2) * step_c + m_lane % 2
    pick_rank = jnp.where((l_row == want) & (m_lane < 8), 1.0, 0.0).astype(BF)
    pick_gate = jnp.where((l_row == want + 64) & (m_lane < 8), 1.0, 0.0).astype(BF)
    rank_col = jnp.dot(info, pick_rank, preferred_element_type=F32)
    gate_col = jnp.dot(info, pick_gate, preferred_element_type=F32)
    m_row = lax.broadcasted_iota(jnp.int32, (16, 128), 0)
    l_lane = lax.broadcasted_iota(jnp.int32, (16, 128), 1)
    pick_row = jnp.where(
        l_lane == base + (m_row // 2) * step_c + m_row % 2, 1.0, 0.0
    ).astype(BF)
    rank_row = lax.dot_general(
        pick_row, info, (((1,), (1,)), ((), ())), preferred_element_type=F32
    )
    src_row = (lax.broadcasted_iota(jnp.int32, (16, 512), 1) // 32).astype(F32)
    code_row = jnp.where(rank_row > -0.5, src_row * 6.0 + rank_row, -1.0)
    src_col = (lax.broadcasted_iota(jnp.int32, (512, 128), 0) // 32).astype(F32)
    code_col = jnp.where(rank_col > -0.5, src_col * 6.0 + rank_col, -1000.0)
    at_row = lax.broadcasted_iota(jnp.int32, (96, 512), 0).astype(F32)
    at_col = lax.broadcasted_iota(jnp.int32, (512, 768), 1).astype(F32)
    weight = jnp.zeros((512, 768), F32)
    for m in range(8):
        pick[m // 2, (m % 2) * 96 : (m % 2 + 1) * 96] = jnp.where(
            at_row == code_row[m : m + 1], 1.0, 0.0
        ).astype(BF)
        weight = weight + jnp.where(
            at_col == code_col[:, m : m + 1] + (96.0 * m), gate_col[:, m : m + 1], 0.0
        )
    give[...] = weight.astype(BF)

    def pass_on(g):
        for i in range(2):
            s2(g, i).wait_recv()
        for i in range(2):
            relay(g, i).start()
        if g + AHEAD < NO:
            second(g + AHEAD)

    def chosen(q, o):
        p = pick[lax.rem(c + o, 4)]
        return [
            jnp.dot(
                p,
                tok[q, :, :, :, n * 256 : (n + 1) * 256].reshape(512, 256),
                preferred_element_type=F32,
            ).astype(BF).reshape(2, 96, 256)
            for n in range(CW // 256)
        ]

    def select(g):
        for i in range(2):
            relay(g, i).wait_recv()

        def others(q):
            def other(i, carry):
                for n, part in enumerate(chosen(q, i + 1)):
                    stage[q, i, :, :, n * 256 : (n + 1) * 256] = part
                return carry

            lax.fori_loop(0, 3, other, 0)

        def own(q):
            for n, part in enumerate(chosen(q, 0)):
                rows[q, 0, :, c, :, n * 256 : (n + 1) * 256] = part

        units(g, others, OUT)
        for i in range(3):
            s3(g, i).start()
        units(g, own, OUT)

    def share(g):
        for i in range(3):
            s3(g, i).wait_recv()
        s4(g).start()

    def up(g, s):
        q, size = OUT[g]
        slot = g % 2

        def one(j, carry):
            for n in range(3):
                cols = slice(n * 256, (n + 1) * 256)
                d = None if g == 0 else acc[s, j, :, cols]
                for u in range(size):
                    r = jnp.dot(
                        rows[q + u, s, j].reshape(384, CW),
                        wgu[slot, j, u * CW : (u + 1) * CW, cols],
                        preferred_element_type=F32,
                    )
                    d = r if d is None else d + r
                acc[s, j, :, cols] = d
            return carry

        lax.fori_loop(0, 2, one, 0)

    for step in range(NO + 3):
        if step < NO:
            pass_on(step)
        if 0 <= step - 1 < NO:
            select(step - 1)
        if 0 <= step - 3 < NO:
            g = step - 3
            s4(g).wait_recv()
            up(g, 1)
            if g + 2 < NO:
                for copy in load_up(g + 2):
                    copy.start()
        if 0 <= step - 2 < NO:
            g = step - 2
            share(g)
            for copy in load_up(g):
                copy.wait()
            up(g, 0)

    def activate(s):
        def one(j, carry):
            v = acc[s, j, :, 0:384]
            hid[s, j] = (v / (1.0 + jnp.exp(-v)) * acc[s, j, :, 384:768]).astype(BF)
            return carry

        lax.fori_loop(0, 2, one, 0)

    def down(q, s, j, n):
        return jnp.dot(
            hid[s, j], wdn[q, j, :, n * 256 : (n + 1) * 256], preferred_element_type=F32
        )

    def down_sibling(q):
        def one(j, carry):
            for n in range(CW // 256):
                rows[q, 1, j, :, :, n * 256 : (n + 1) * 256] = (
                    down(q, 1, j, n).astype(BF).reshape(4, 96, 256)
                )
            return carry

        lax.fori_loop(0, 2, one, 0)

    def down_own(q):
        def one(j, carry):
            for n in range(CW // 256):
                cols = slice(n * 256, (n + 1) * 256)
                v = down(q, 0, j, n).reshape(4, 96, 256) + back[q, j, :, :, cols].astype(F32)
                rows[q, 0, j, :, :, cols] = v.astype(BF)
            return carry

        lax.fori_loop(0, 2, one, 0)
        zin[q, c] = rows[q, 0, :, c]

    activate(1)
    for g in range(NO):
        s4(g).wait_send()
        for i in range(2):
            s2(g, i).wait_send()
            relay(g, i).wait_send()
        for i in range(3):
            s3(g, i).wait_send()
    for step in range(NH + 1):
        if step < NH:
            q, n = HOME[step]
            for u in range(q, q + n):
                load_down(u).wait()
            units(step, down_sibling)
            yb(step).start()
        if step == 0:
            activate(0)
        if step >= 1:
            g = step - 1
            yb(g).wait_recv()
            units(g, down_own)
            if g < BACK:
                for i in range(3):
                    b3(g, i).start()

    def one_sum(q, o):
        y_ = Ys[o]
        g = give[pl.ds(pl.multiple_of(y_ * 128, 128), 128)]
        for n in range(CW // 256):
            cols = slice(n * 256, (n + 1) * 256)
            tok[q, y_, :, :, cols] = jnp.dot(
                g, zin[q, :, :, :, cols].reshape(768, 256), preferred_element_type=F32
            ).astype(BF).reshape(4, 32, 256)

    def gather_sums(g):
        for i in range(3):
            b3(g, i).wait_recv()
        if g + BACK < NH:
            for i in range(3):
                b3(g + BACK, i).start()
        units(g, lambda q: one_sum(q, 2))
        for i in range(2):
            far(g, i).start()

        def rest(q):
            for o in (1, 3, 0):
                one_sum(q, o)

        units(g, rest)

    def add_half(g):
        for i in range(2):
            far(g, i).wait_recv()

            def add(q):
                block = tok[q, Yn[i], parts[i]].astype(F32) + uhalf[q, i].astype(F32)
                tok[q, Yn[i], parts[i]] = block.astype(BF)

            units(g, add)
            b2(g, i).start()

    def along(g):
        for i in range(2):
            b2(g, i).wait_recv()

        def add(q):
            v = uin[q, 0].astype(F32) + uin[q, 1].astype(F32) + tok[q, y].astype(F32)
            vout[q] = v.astype(BF)
            vin[q, a] = vout[q, a]

        units(g, add)
        for i in range(3):
            b1(g, i).start()

    def store(g):
        for i in range(3):
            b1(g, i).wait_recv()

        def add(q):
            v = vin[q, 0].astype(F32) + vin[q, 1].astype(F32)
            v = v + vin[q, 2].astype(F32) + vin[q, 3].astype(F32)
            cols = pl.ds(pl.multiple_of(q * CW, CW), CW)
            out_ref[:, cols] = (hsum_ref[q] + v).astype(BF)

        units(g, add)

    for step in range(NH + 3):
        if 0 <= step - 1 < NH:
            add_half(step - 1)
        if step < NH:
            gather_sums(step)
        if 0 <= step - 2 < NH:
            along(step - 2)
        if 0 <= step - 3 < NH:
            store(step - 3)

    for g in range(NH):
        yb(g).wait_send()
        for i in range(3):
            b3(g, i).wait_send()
            b1(g, i).wait_send()
        for i in range(2):
            far(g, i).wait_send()
            b2(g, i).wait_send()


def mixture(normed, hsum, routes, gates, w_gate, w_up, w_down):
    dma = pltpu.SemaphoreType.DMA
    vm = pl.BlockSpec(memory_space=pltpu.VMEM)
    hbm = pl.BlockSpec(memory_space=pl.ANY)
    return pl.pallas_call(
        experts_kernel,
        out_shape=jax.ShapeDtypeStruct((32, D), BF),
        in_specs=[vm] * 4 + [hbm] * 3,
        out_specs=vm,
        scratch_shapes=[
            pltpu.VMEM((CH, 4, 4, 32, CW), BF),
            pltpu.VMEM((4, 4, 32, 128), BF),
            pltpu.VMEM((CH, 3, 2, 96, CW), BF),
            pltpu.VMEM((CH, 2, 2, 4, 96, CW), BF),
            pltpu.VMEM((2, 2, 384, 768), F32),
            pltpu.VMEM((2, 2, 384, 384), BF),
            pltpu.VMEM((2, 2, 2 * CW, 768), BF),
            pltpu.VMEM((CH, 2, 384, CW), BF),
            pltpu.VMEM((CH, 2, 4, 96, CW), BF),
            pltpu.VMEM((CH, 4, 2, 96, CW), BF),
            pltpu.VMEM((CH, 2, 4, 32, CW), BF),
            pltpu.VMEM((CH, 2, 2, 32, CW), BF),
            pltpu.VMEM((CH, 4, 32, CW), BF),
            pltpu.VMEM((CH, 4, 32, CW), BF),
            pltpu.VMEM((4, 192, 512), BF),
            pltpu.VMEM((512, 768), BF),
            dma((6,)), dma((6,)),
            dma((NO, 3)), dma((NO, 3)), dma((NO, 4)), dma((NO, 4)), dma((NO, 3)), dma((NO, 3)),
            dma((NO,)), dma((NO,)), dma((NH,)), dma((NH,)),
            dma((NH, 3)), dma((NH, 3)), dma((NH, 4)), dma((NH, 4)), dma((NH, 3)), dma((NH, 3)),
            dma((2,)), dma((2,)), dma((CH,)),
        ],
        compiler_params=pltpu.CompilerParams(
            collective_id=1, has_side_effects=True, vmem_limit_bytes=63 * 2**20
        ),
        cost_estimate=pl.CostEstimate(
            flops=20 * 10**9, bytes_accessed=20 * 2**20, transcendentals=2**20
        ),
    )(normed, hsum, routes.T, gates.T, w_gate, w_up, w_down)


def shards(
    queries, keys, values, resid, out_weight, norm_gain, routes, gates, w_gate, w_up, w_down
):
    hsum, normed = attention(queries, keys, values, out_weight, resid, norm_gain)
    return mixture(normed, hsum, routes, gates, w_gate, w_up, w_down)


def solution(mesh):
    return jax.shard_map(
        shards,
        mesh=mesh,
        in_specs=(
            P("context", "tensor"),
            P("context", "tensor"),
            P("context", "tensor"),
            P(("context", "tensor"), None),
            P("tensor", "context"),
            P(),
            P(("context", "tensor"), None),
            P(("context", "tensor"), None),
            P("context", None, "tensor"),
            P("context", None, "tensor"),
            P("context", "tensor", None),
        ),
        out_specs=P(("context", "tensor"), None),
        check_vma=False,
    )
```

```python
import functools
import jax
import jax.numpy as jnp
from jax import lax
from jax.experimental import pallas as pl
from jax.experimental.pallas import tpu as pltpu
from jax.sharding import PartitionSpec as P

D = 4096
HW = 128
MESH = pl.DeviceIdType.MESH
BF = jnp.bfloat16
F32 = jnp.float32


def place():
    c = lax.axis_index("context")
    t = lax.axis_index("tensor")
    return c // 8, (c // 2) % 4, c % 2, t // 2, t % 2


def device(z, x, yl, yh, core):
    return {"context": z * 8 + x * 2 + yl, "tensor": yh * 2 + core}


def send(src, dst, ssem, rsem, to):
    copy = pltpu.make_async_remote_copy(
        src_ref=src, dst_ref=dst, send_sem=ssem, recv_sem=rsem, device_id=to, device_id_type=MESH
    )
    copy.start()
    return copy


def greet(peers):
    barrier = pltpu.get_barrier_semaphore()
    for peer in peers:
        pl.semaphore_signal(barrier, inc=1, device_id=peer, device_id_type=MESH)
    pl.semaphore_wait(barrier, len(peers))


def attention_kernel(
    q_ref, k_ref, v_ref, w_ref, resid_ref, gain_ref, hsum_ref, normed_ref,
    kall, vall, wall, att, scores, acc, sib_out, sib_in, own_out, own_in,
    k_s, k_r, v_s, v_r, w_s, w_r, a_s, a_r, c_s, c_r, o_s, o_r,
):
    z, x, yl, yh, core = place()
    ctx = z * 8 + x * 2 + yl
    zs = [lax.rem(z + o, 4) for o in range(4)]
    xs = [lax.rem(x + o, 4) for o in range(4)]
    group = [(o, p) for o in range(4) for p in range(2)][1:]
    sibling = device(z, x, yl, yh, 1 - core)
    z_peers = [device(zs[o], x, yl, yh, core) for o in (1, 2, 3)]
    x_peers = [device(z, xs[o], yl, yh, core) for o in (1, 2, 3)]
    y_peer = device(z, x, 1 - yl, yh, core)
    o_peers = [device(zs[o], x, yl, lax.rem(yh + p, 2), core) for o, p in group]
    greet([sibling, y_peer] + z_peers + x_peers + [device(zs[o], x, yl, 1 - yh, core) for o in range(4)])

    kall[z, x, yl] = k_ref[...]
    vall[z, x, yl] = v_ref[...]
    me = (z, x, yl)
    mine = pl.ds(pl.multiple_of((x * 2 + yl) * 128, 128), 128)
    both = pl.ds(pl.multiple_of(x * 256, 256), 256)
    low, high = pl.ds(0, 896), pl.ds(896, 1152)
    wall[:, mine] = w_ref[...]

    def wa1():
        return [send(w_ref.at[low], wall.at[low, mine], w_s.at[0], w_r.at[0], y_peer)]

    def wb1():
        return [
            send(w_ref.at[high], wall.at[high, mine], w_s.at[1 + i], w_r.at[1 + i], x_peers[i])
            for i in range(3)
        ]

    k1 = [send(kall.at[me], kall.at[me], k_s.at[i], k_r.at[i], z_peers[i]) for i in range(3)]
    v1 = [send(vall.at[me], vall.at[me], v_s.at[0], v_r.at[0], y_peer)]
    for copy in v1:
        copy.wait_recv()
    v2 = [
        send(vall.at[z, x], vall.at[z, x], v_s.at[1 + i], v_r.at[1 + i], x_peers[i])
        for i in range(3)
    ]
    v3 = []
    k3 = []

    def v_on(p, x_):
        for i in range(3):
            n = 4 + 3 * p + i
            v3.append(send(vall.at[z, x_], vall.at[z, x_], v_s.at[n], v_r.at[n], z_peers[i]))

    def k_on(p, x_):
        n = 6 + p
        k3.append(send(kall.at[:, x_, yl], kall.at[:, x_, yl], k_s.at[n], k_r.at[n], y_peer))

    v_on(0, x)
    for copy in k1:
        copy.wait_recv()
    k2 = [
        send(kall.at[:, x, yl], kall.at[:, x, yl], k_s.at[3 + i], k_r.at[3 + i], x_peers[i])
        for i in range(3)
    ]
    k_on(0, x)
    for i in range(3):
        x_ = lax.rem(x + 3 - i, 4)
        v2[i].wait_recv()
        v_on(1 + i, x_)
        k2[i].wait_recv()
        k_on(1 + i, x_)
    w1 = wb1() + wa1()
    w2 = []

    def wb2(p, x_):
        cols = pl.ds(pl.multiple_of((x_ * 2 + yl) * 128, 128), 128)
        w2.append(send(wall.at[high, cols], wall.at[high, cols], w_s.at[7 + p], w_r.at[7 + p], y_peer))

    wb2(0, x)
    for copy in v3 + k3:
        copy.wait_recv()

    def forward():
        for i in range(3):
            w1[i].wait_recv()
            wb2(1 + i, lax.rem(x + 3 - i, 4))
        w1[3].wait_recv()
        for i in range(3):
            w2.append(
                send(
                    wall.at[low, both], wall.at[low, both], w_s.at[4 + i], w_r.at[4 + i], x_peers[i]
                )
            )

    factor = HW**-0.5 * 1.4426950408889634
    last = ctx // 4
    nrow = 512

    def keys_of(ref, ch):
        return ref[ch // 2, pl.ds((ch % 2) * 2, 2)].reshape(512, HW)

    def columns(ch):
        return pl.ds(pl.multiple_of(ch * 512, 512), 512)

    def fold(f, s):
        return f(f(s[:, 0:128], s[:, 128:256]), f(s[:, 256:384], s[:, 384:512]))

    def heads(hc, carry):
        q = jnp.concatenate(
            [
                q_ref[:, pl.ds(pl.multiple_of(hc * 512 + i * HW, HW), HW)]
                for i in range(4)
            ],
            axis=0,
        )

        def product(ch):
            return lax.dot_general(
                q, keys_of(kall, ch), (((1,), (1,)), ((), ())), preferred_element_type=F32
            )

        def first(ch, top):
            s = product(ch)
            scores[:, columns(ch)] = s
            return jnp.maximum(top, fold(jnp.maximum, s))

        top = lax.fori_loop(0, last, first, jnp.full((nrow, 128), -jnp.inf, F32))
        s = product(last)
        row = lax.broadcasted_iota(jnp.int32, (nrow, 512), 0) % 128
        col = lax.broadcasted_iota(jnp.int32, (nrow, 512), 1)
        s = jnp.where(col <= row + (ctx % 4) * 128, s, -jnp.inf)
        scores[:, columns(last)] = s
        top = jnp.maximum(top, fold(jnp.maximum, s))
        shift = jnp.max(top, axis=1, keepdims=True) * factor

        def second(ch, carry):
            total, summed = carry
            p = jnp.exp2(scores[:, columns(ch)] * factor - shift)
            total = total + fold(jnp.add, p)
            summed = summed + jnp.dot(p.astype(BF), keys_of(vall, ch), preferred_element_type=F32)
            return total, summed

        zero = jnp.zeros((nrow, 128), F32)
        total, summed = lax.fori_loop(0, last + 1, second, (zero, zero))
        out = (summed / jnp.sum(total, axis=1, keepdims=True)).astype(BF)
        for i in range(4):
            att[z, hc, :, i * HW : (i + 1) * HW] = out[i * 128 : (i + 1) * 128]
        for i in range(3):
            send(att.at[z, hc], att.at[z, hc], a_s.at[hc, i], a_r.at[hc, i], z_peers[i])
        return carry

    lax.fori_loop(0, 1, heads, 0)
    forward()
    lax.fori_loop(1, 4, heads, 0)
    for copy in w2:
        copy.wait_recv()

    def project(hc, carry):
        for i in range(3):
            pltpu.make_async_remote_copy(
                src_ref=att.at[z, hc], dst_ref=att.at[z, hc], send_sem=a_s.at[hc, i],
                recv_sem=a_r.at[hc, i], device_id=z_peers[i], device_id_type=MESH,
            ).wait()
        a = att[:, hc].reshape(512, 512)
        for n in range(4):
            cols = slice(n * 256, (n + 1) * 256)
            r = jnp.dot(
                a, wall[pl.ds(pl.multiple_of(hc * 512, 512), 512), cols], preferred_element_type=F32
            ).reshape(4, 2, 2, 32, 256)
            acc[:, :, :, :, cols] = jnp.where(hc == 0, r, acc[:, :, :, :, cols] + r)
        return carry

    acc[...] = jnp.zeros_like(acc)
    lax.fori_loop(0, 4, project, 0)
    sib_out[...] = acc[:, :, 1 - core].astype(BF)
    copy = send(sib_out, sib_in, c_s.at[0], c_r.at[0], sibling)
    copy.wait()
    own_out[...] = (acc[:, :, core] + sib_in[...].astype(F32)).astype(BF)
    ocopies = []
    for i, (o, p) in enumerate(group):
        ocopies.append(
            send(
                own_out.at[zs[o], lax.rem(yh + p, 2)], own_in.at[z, yh], o_s.at[i], o_r.at[i], o_peers[i]
            )
        )
    own_in[z, yh] = own_out[z, yh]
    for copy in ocopies:
        copy.wait()
    square = jnp.zeros((32, 1), F32)
    for n in range(8):
        at, cols = n // 2, slice((n % 2) * 512, (n % 2 + 1) * 512)
        h = resid_ref[:, n * 512 : (n + 1) * 512].astype(F32) + (
            own_in[at, 0, :, cols].astype(F32) + own_in[at, 1, :, cols].astype(F32)
        )
        hsum_ref[n] = h
        square = square + jnp.sum(h * h, axis=1, keepdims=True)
    scale = lax.rsqrt(square * (1.0 / D) + 1e-06)
    for n in range(8):
        normed_ref[n] = (hsum_ref[n] * scale * gain_ref[:, n * 512 : (n + 1) * 512]).astype(BF)
    for copy in k1 + k2 + k3 + v1 + v2 + v3 + w1 + w2:
        copy.wait_send()


def attention(queries, keys, values, out_weight, resid, norm_gain):
    dma = pltpu.SemaphoreType.DMA
    vm = pl.BlockSpec(memory_space=pltpu.VMEM)
    return pl.pallas_call(
        attention_kernel,
        out_shape=(
            jax.ShapeDtypeStruct((8, 32, 512), F32),
            jax.ShapeDtypeStruct((8, 32, 512), BF),
        ),
        in_specs=[vm] * 6,
        out_specs=(vm, vm),
        scratch_shapes=[
            pltpu.VMEM((4, 4, 2, 128, 128), BF),
            pltpu.VMEM((4, 4, 2, 128, 128), BF),
            pltpu.VMEM((2048, 1024), BF),
            pltpu.VMEM((4, 4, 128, 512), BF),
            pltpu.VMEM((512, 4096), F32),
            pltpu.VMEM((4, 2, 2, 32, 1024), F32),
            pltpu.VMEM((4, 2, 32, 1024), BF),
            pltpu.VMEM((4, 2, 32, 1024), BF),
            pltpu.VMEM((4, 2, 32, 1024), BF),
            pltpu.VMEM((4, 2, 32, 1024), BF),
            dma((10,)), dma((10,)), dma((16,)), dma((16,)), dma((11,)), dma((11,)),
            dma((4, 3)), dma((4, 3)), dma((1,)), dma((1,)), dma((7,)), dma((7,)),
        ],
        compiler_params=pltpu.CompilerParams(
            collective_id=0, has_side_effects=True, vmem_limit_bytes=56 * 2**20
        ),
        cost_estimate=pl.CostEstimate(flops=8 * 10**9, bytes_accessed=4 * 2**20, transcendentals=8 * 2**20),
    )(queries, keys, values, out_weight, resid, norm_gain.reshape(1, D))


CH = 8
CW = D // CH
OUT = tuple((q, 1) for q in range(8))
HOME = ((0, 2), (2, 2), (4, 2), (6, 2))
NO, NH = len(OUT), len(HOME)
AHEAD = 2
BACK = 2


def experts_kernel(
    normed_ref, hsum_ref, routes_ref, gates_ref, wg_ref, wu_ref, wd_ref, out_ref,
    tok, meta, stage, rows, acc, hid, wgu, wdn, back, zin, uin, uhalf, vout, vin, pick, give,
    m_s, m_r, s1_s, s1_r, s2_s, s2_r, s3_s, s3_r, s4_s, s4_r,
    y_s, y_r, b3_s, b3_r, b2_s, b2_r, b1_s, b1_r, wg_m, wu_m, wd_m,
):
    z, x, yl, yh, core = place()
    y = yh * 2 + yl
    a = z * (1 - core) + x * core
    c = x * (1 - core) + z * core

    def at(a_, y_, c_):
        return device(
            a_ * (1 - core) + c_ * core, c_ * (1 - core) + a_ * core, y_ % 2, y_ // 2, core
        )

    As = [lax.rem(a + o, 4) for o in range(4)]
    Ys = [lax.rem(y + o, 4) for o in range(4)]
    Cs = [lax.rem(c + o, 4) for o in range(4)]
    a_peers = [at(As[o], y, c) for o in (1, 2, 3)]
    y_peers = [at(a, Ys[o], c) for o in (1, 2, 3)]
    c_peers = [at(a, y, Cs[o]) for o in (1, 2, 3)]
    sibling = device(z, x, yl, yh, 1 - core)
    greet([sibling] + a_peers + y_peers + c_peers)

    def un(g, groups=OUT):
        return pl.ds(*groups[g])

    def remote(src, dst, ssem, rsem, to):
        return pltpu.make_async_remote_copy(
            src_ref=src, dst_ref=dst, send_sem=ssem, recv_sem=rsem, device_id=to, device_id_type=MESH
        )

    def m1(i):
        return remote(meta.at[y, a], meta.at[y, a], m_s.at[i], m_r.at[i], a_peers[i])

    def m2(i):
        return remote(meta.at[y], meta.at[y], m_s.at[3 + i], m_r.at[3 + i], y_peers[i])

    def s1(g, i):
        u = un(g)
        return remote(normed_ref.at[u], tok.at[u, y, a], s1_s.at[g, i], s1_r.at[g, i], a_peers[i])

    ends = (y_peers[0], y_peers[2])
    Yn = (Ys[1], Ys[3])
    parts = (pl.ds(0, 2), pl.ds(2, 2))

    def s2(g, i):
        block = tok.at[un(g), y]
        return remote(block, block, s2_s.at[g, i], s2_r.at[g, i], ends[i])

    def relay(g, i):
        block = tok.at[un(g), Yn[1 - i], parts[i]]
        return remote(block, block, s2_s.at[g, 2 + i], s2_r.at[g, 2 + i], ends[i])

    def s3(g, i):
        u = un(g)
        return remote(
            stage.at[u, i], rows.at[u, 0, :, c], s3_s.at[g, i], s3_r.at[g, i], c_peers[i]
        )

    def s4(g):
        u = un(g)
        return remote(rows.at[u, 0], rows.at[u, 1], s4_s.at[g], s4_r.at[g], sibling)

    def yb(g):
        u = un(g, HOME)
        return remote(rows.at[u, 1], back.at[u], y_s.at[g], y_r.at[g], sibling)

    def b3(g, i):
        u = un(g, HOME)
        return remote(
            rows.at[u, 0, :, Cs[i + 1]], zin.at[u, c], b3_s.at[g, i], b3_r.at[g, i], c_peers[i]
        )

    def b2(g, i):
        u = un(g, HOME)
        return remote(tok.at[u, Yn[i]], uin.at[u, i], b2_s.at[g, i], b2_r.at[g, i], ends[i])

    def far(g, i):
        u = un(g, HOME)
        block = tok.at[u, Ys[2], parts[i]]
        return remote(block, uhalf.at[u, i], b2_s.at[g, 2 + i], b2_r.at[g, 2 + i], ends[i])

    def b1(g, i):
        u = un(g, HOME)
        return remote(vout.at[u, As[i + 1]], vin.at[u, a], b1_s.at[g, i], b1_r.at[g, i], a_peers[i])

    def units(g, body, groups=HOME):
        q, n = groups[g]

        def one(u, carry):
            body(u)
            return carry

        if n == 1:
            body(q)
        else:
            lax.fori_loop(q, q + n, one, 0)

    def load_up(g):
        q, n = OUT[g]
        slot, depth, held = g % 2, pl.ds(q * CW, n * CW), pl.ds(0, n * CW)
        return (
            pltpu.make_async_copy(wg_ref.at[:, depth], wgu.at[slot, :, held, 0:384], wg_m.at[slot]),
            pltpu.make_async_copy(
                wu_ref.at[:, depth], wgu.at[slot, :, held, 384:768], wu_m.at[slot]
            ),
        )

    def load_down(q):
        return pltpu.make_async_copy(
            wd_ref.at[:, :, q * CW : (q + 1) * CW], wdn.at[q], wd_m.at[q]
        )

    lane = lax.broadcasted_iota(jnp.int32, (32, 128), 1)
    expert = (lane % 64).astype(F32)
    same = lax.broadcasted_iota(jnp.int32, (32, 32), 0) == lax.broadcasted_iota(
        jnp.int32, (32, 32), 1
    )
    turn = jnp.where(same, 1.0, 0.0).astype(BF)
    across = (((1,), (1,)), ((), ()))
    route_col = lax.dot_general(
        turn, routes_ref[...].astype(F32).astype(BF), across, preferred_element_type=F32
    )
    gate_own = lax.dot_general(
        turn, gates_ref[...].astype(BF), across, preferred_element_type=F32
    )
    named = jnp.zeros((32, 128), F32)
    gate = jnp.zeros((32, 128), F32)
    for k in range(8):
        hit = route_col[:, k : k + 1] == expert
        named = named + jnp.where(hit, 1.0, 0.0)
        gate = gate + jnp.where(hit, gate_own[:, k : k + 1], 0.0)
    before = (
        lax.broadcasted_iota(jnp.int32, (32, 32), 1) < lax.broadcasted_iota(jnp.int32, (32, 32), 0)
    )
    rank = jnp.dot(
        jnp.where(before, 1.0, 0.0).astype(BF), named.astype(BF), preferred_element_type=F32
    )
    meta[y, a] = jnp.where(lane < 64, jnp.where(named > 0.5, rank, -1.0), gate).astype(BF)
    tok[:, y, a] = normed_ref[...]
    for i in range(3):
        s1(0, i).start()
    for i in range(3):
        m1(i).start()
    for g in range(2):
        for copy in load_up(g):
            copy.start()
    for q in range(CH):
        load_down(q).start()

    def second(g):
        for i in range(3):
            s1(g, i).wait()
        for i in range(2):
            s2(g, i).start()

    second(0)
    for g in range(1, NO):
        for i in range(3):
            s1(g, i).start()
    for i in range(3):
        m1(i).wait()
    for i in range(3):
        m2(i).start()
    for g in range(1, AHEAD):
        second(g)
    for i in range(3):
        m2(i).wait()

    info = meta[...].reshape(512, 128)
    base = a * (16 * (1 - core) + 4 * core) + 2 * yl
    step_c = 4 * (1 - core) + 16 * core
    m_lane = lax.broadcasted_iota(jnp.int32, (128, 128), 1)
    l_row = lax.broadcasted_iota(jnp.int32, (128, 128), 0)
    want = base + (m_lane // 2) * step_c + m_lane % 2
    pick_rank = jnp.where((l_row == want) & (m_lane < 8), 1.0, 0.0).astype(BF)
    pick_gate = jnp.where((l_row == want + 64) & (m_lane < 8), 1.0, 0.0).astype(BF)
    rank_col = jnp.dot(info, pick_rank, preferred_element_type=F32)
    gate_col = jnp.dot(info, pick_gate, preferred_element_type=F32)
    m_row = lax.broadcasted_iota(jnp.int32, (16, 128), 0)
    l_lane = lax.broadcasted_iota(jnp.int32, (16, 128), 1)
    pick_row = jnp.where(
        l_lane == base + (m_row // 2) * step_c + m_row % 2, 1.0, 0.0
    ).astype(BF)
    rank_row = lax.dot_general(
        pick_row, info, (((1,), (1,)), ((), ())), preferred_element_type=F32
    )
    src_row = (lax.broadcasted_iota(jnp.int32, (16, 512), 1) // 32).astype(F32)
    code_row = jnp.where(rank_row > -0.5, src_row * 6.0 + rank_row, -1.0)
    src_col = (lax.broadcasted_iota(jnp.int32, (512, 128), 0) // 32).astype(F32)
    code_col = jnp.where(rank_col > -0.5, src_col * 6.0 + rank_col, -1000.0)
    at_row = lax.broadcasted_iota(jnp.int32, (96, 512), 0).astype(F32)
    at_col = lax.broadcasted_iota(jnp.int32, (512, 768), 1).astype(F32)
    weight = jnp.zeros((512, 768), F32)
    for m in range(8):
        pick[m // 2, (m % 2) * 96 : (m % 2 + 1) * 96] = jnp.where(
            at_row == code_row[m : m + 1], 1.0, 0.0
        ).astype(BF)
        weight = weight + jnp.where(
            at_col == code_col[:, m : m + 1] + (96.0 * m), gate_col[:, m : m + 1], 0.0
        )
    give[...] = weight.astype(BF)

    def pass_on(g):
        for i in range(2):
            s2(g, i).wait_recv()
        for i in range(2):
            relay(g, i).start()
        if g + AHEAD < NO:
            second(g + AHEAD)

    def chosen(q, o):
        p = pick[lax.rem(c + o, 4)]
        return [
            jnp.dot(
                p,
                tok[q, :, :, :, n * 256 : (n + 1) * 256].reshape(512, 256),
                preferred_element_type=F32,
            ).astype(BF).reshape(2, 96, 256)
            for n in range(CW // 256)
        ]

    def select(g):
        for i in range(2):
            relay(g, i).wait_recv()

        def others(q):
            def other(i, carry):
                for n, part in enumerate(chosen(q, i + 1)):
                    stage[q, i, :, :, n * 256 : (n + 1) * 256] = part
                return carry

            lax.fori_loop(0, 3, other, 0)

        def own(q):
            for n, part in enumerate(chosen(q, 0)):
                rows[q, 0, :, c, :, n * 256 : (n + 1) * 256] = part

        units(g, others, OUT)
        for i in range(3):
            s3(g, i).start()
        units(g, own, OUT)

    def share(g):
        for i in range(3):
            s3(g, i).wait_recv()
        s4(g).start()

    def up(g, s):
        q, size = OUT[g]
        slot = g % 2

        def one(j, carry):
            for n in range(3):
                cols = slice(n * 256, (n + 1) * 256)
                d = None if g == 0 else acc[s, j, :, cols]
                for u in range(size):
                    r = jnp.dot(
                        rows[q + u, s, j].reshape(384, CW),
                        wgu[slot, j, u * CW : (u + 1) * CW, cols],
                        preferred_element_type=F32,
                    )
                    d = r if d is None else d + r
                acc[s, j, :, cols] = d
            return carry

        lax.fori_loop(0, 2, one, 0)

    for step in range(NO + 3):
        if step < NO:
            pass_on(step)
        if 0 <= step - 1 < NO:
            select(step - 1)
        if 0 <= step - 3 < NO:
            g = step - 3
            s4(g).wait_recv()
            up(g, 1)
            if g + 2 < NO:
                for copy in load_up(g + 2):
                    copy.start()
        if 0 <= step - 2 < NO:
            g = step - 2
            share(g)
            for copy in load_up(g):
                copy.wait()
            up(g, 0)

    def activate(s):
        def one(j, carry):
            v = acc[s, j, :, 0:384]
            hid[s, j] = (v / (1.0 + jnp.exp(-v)) * acc[s, j, :, 384:768]).astype(BF)
            return carry

        lax.fori_loop(0, 2, one, 0)

    def down(q, s, j, n):
        return jnp.dot(
            hid[s, j], wdn[q, j, :, n * 256 : (n + 1) * 256], preferred_element_type=F32
        )

    def down_sibling(q):
        def one(j, carry):
            for n in range(CW // 256):
                rows[q, 1, j, :, :, n * 256 : (n + 1) * 256] = (
                    down(q, 1, j, n).astype(BF).reshape(4, 96, 256)
                )
            return carry

        lax.fori_loop(0, 2, one, 0)

    def down_own(q):
        def one(j, carry):
            for n in range(CW // 256):
                cols = slice(n * 256, (n + 1) * 256)
                v = down(q, 0, j, n).reshape(4, 96, 256) + back[q, j, :, :, cols].astype(F32)
                rows[q, 0, j, :, :, cols] = v.astype(BF)
            return carry

        lax.fori_loop(0, 2, one, 0)
        zin[q, c] = rows[q, 0, :, c]

    activate(1)
    for g in range(NO):
        s4(g).wait_send()
        for i in range(2):
            s2(g, i).wait_send()
            relay(g, i).wait_send()
        for i in range(3):
            s3(g, i).wait_send()
    for step in range(NH + 1):
        if step < NH:
            q, n = HOME[step]
            for u in range(q, q + n):
                load_down(u).wait()
            units(step, down_sibling)
            yb(step).start()
        if step == 0:
            activate(0)
        if step >= 1:
            g = step - 1
            yb(g).wait_recv()
            units(g, down_own)
            if g < BACK:
                for i in range(3):
                    b3(g, i).start()

    def one_sum(q, o):
        y_ = Ys[o]
        g = give[pl.ds(pl.multiple_of(y_ * 128, 128), 128)]
        for n in range(CW // 256):
            cols = slice(n * 256, (n + 1) * 256)
            tok[q, y_, :, :, cols] = jnp.dot(
                g, zin[q, :, :, :, cols].reshape(768, 256), preferred_element_type=F32
            ).astype(BF).reshape(4, 32, 256)

    def gather_sums(g):
        for i in range(3):
            b3(g, i).wait_recv()
        if g + BACK < NH:
            for i in range(3):
                b3(g + BACK, i).start()
        units(g, lambda q: one_sum(q, 2))
        for i in range(2):
            far(g, i).start()

        def rest(q):
            for o in (1, 3, 0):
                one_sum(q, o)

        units(g, rest)

    def add_half(g):
        for i in range(2):
            far(g, i).wait_recv()

            def add(q):
                block = tok[q, Yn[i], parts[i]].astype(F32) + uhalf[q, i].astype(F32)
                tok[q, Yn[i], parts[i]] = block.astype(BF)

            units(g, add)
            b2(g, i).start()

    def along(g):
        for i in range(2):
            b2(g, i).wait_recv()

        def add(q):
            v = uin[q, 0].astype(F32) + uin[q, 1].astype(F32) + tok[q, y].astype(F32)
            vout[q] = v.astype(BF)
            vin[q, a] = vout[q, a]

        units(g, add)
        for i in range(3):
            b1(g, i).start()

    def store(g):
        for i in range(3):
            b1(g, i).wait_recv()

        def add(q):
            v = vin[q, 0].astype(F32) + vin[q, 1].astype(F32)
            v = v + vin[q, 2].astype(F32) + vin[q, 3].astype(F32)
            cols = pl.ds(pl.multiple_of(q * CW, CW), CW)
            out_ref[:, cols] = (hsum_ref[q] + v).astype(BF)

        units(g, add)

    for step in range(NH + 3):
        if 0 <= step - 1 < NH:
            add_half(step - 1)
        if step < NH:
            gather_sums(step)
        if 0 <= step - 2 < NH:
            along(step - 2)
        if 0 <= step - 3 < NH:
            store(step - 3)

    for g in range(NH):
        yb(g).wait_send()
        for i in range(3):
            b3(g, i).wait_send()
            b1(g, i).wait_send()
        for i in range(2):
            far(g, i).wait_send()
            b2(g, i).wait_send()


def mixture(normed, hsum, routes, gates, w_gate, w_up, w_down):
    dma = pltpu.SemaphoreType.DMA
    vm = pl.BlockSpec(memory_space=pltpu.VMEM)
    hbm = pl.BlockSpec(memory_space=pl.ANY)
    return pl.pallas_call(
        experts_kernel,
        out_shape=jax.ShapeDtypeStruct((32, D), BF),
        in_specs=[vm] * 4 + [hbm] * 3,
        out_specs=vm,
        scratch_shapes=[
            pltpu.VMEM((CH, 4, 4, 32, CW), BF),
            pltpu.VMEM((4, 4, 32, 128), BF),
            pltpu.VMEM((CH, 3, 2, 96, CW), BF),
            pltpu.VMEM((CH, 2, 2, 4, 96, CW), BF),
            pltpu.VMEM((2, 2, 384, 768), F32),
            pltpu.VMEM((2, 2, 384, 384), BF),
            pltpu.VMEM((2, 2, 2 * CW, 768), BF),
            pltpu.VMEM((CH, 2, 384, CW), BF),
            pltpu.VMEM((CH, 2, 4, 96, CW), BF),
            pltpu.VMEM((CH, 4, 2, 96, CW), BF),
            pltpu.VMEM((CH, 2, 4, 32, CW), BF),
            pltpu.VMEM((CH, 2, 2, 32, CW), BF),
            pltpu.VMEM((CH, 4, 32, CW), BF),
            pltpu.VMEM((CH, 4, 32, CW), BF),
            pltpu.VMEM((4, 192, 512), BF),
            pltpu.VMEM((512, 768), BF),
            dma((6,)), dma((6,)),
            dma((NO, 3)), dma((NO, 3)), dma((NO, 4)), dma((NO, 4)), dma((NO, 3)), dma((NO, 3)),
            dma((NO,)), dma((NO,)), dma((NH,)), dma((NH,)),
            dma((NH, 3)), dma((NH, 3)), dma((NH, 4)), dma((NH, 4)), dma((NH, 3)), dma((NH, 3)),
            dma((2,)), dma((2,)), dma((CH,)),
        ],
        compiler_params=pltpu.CompilerParams(
            collective_id=1, has_side_effects=True, vmem_limit_bytes=63 * 2**20
        ),
        cost_estimate=pl.CostEstimate(
            flops=20 * 10**9, bytes_accessed=20 * 2**20, transcendentals=2**20
        ),
    )(normed, hsum, routes.T, gates.T, w_gate, w_up, w_down)


def shards(
    queries, keys, values, resid, out_weight, norm_gain, routes, gates, w_gate, w_up, w_down
):
    hsum, normed = attention(queries, keys, values, out_weight, resid, norm_gain)
    return mixture(normed, hsum, routes, gates, w_gate, w_up, w_down)


def solution(mesh):
    return jax.shard_map(
        shards,
        mesh=mesh,
        in_specs=(
            P("context", "tensor"),
            P("context", "tensor"),
            P("context", "tensor"),
            P(("context", "tensor"), None),
            P("tensor", "context"),
            P(),
            P(("context", "tensor"), None),
            P(("context", "tensor"), None),
            P("context", None, "tensor"),
            P("context", None, "tensor"),
            P("context", "tensor", None),
        ),
        out_specs=P(("context", "tensor"), None),
        check_vma=False,
    )
```
